256 devices in a mesh: bg: 4 (over z_hi), pw: 64 (over y, z_lo, x, core).
Axes of the slice: x: 4, y: 4, z: 8 (z_hi: 4, z_lo: 2; z = z_hi * 2 + z_lo), core: 2. Of those that a mesh axis runs over, the one named last changes fastest.
Arguments:
- orbitals: float32 [8, 4096, 256], P('bg', 'pw'), may hold values from -6 to 6
- applied_orbitals: float32 [8, 4096, 256], P('bg', 'pw'), may hold values from -6 to 6
- potential: float32 [320, 320, 320], P('pw'), may hold values from -6 to 6
- stick_map: int32 [4096], replicated, may hold values from 0 to 16383, as said below
- ritz_values: float32 [8], P('bg'), may hold values from -1 to 1
- ritz_rotation: float32 [16, 8], replicated, may hold values from -1.5 to 1.5
Outputs:
- next_orbitals: float32 [8, 4096, 256], P('bg', 'pw')
- applied_correction: float32 [8, 4096, 256], P('bg', 'pw')
The draws below stay inside these ranges and needn't reach their ends.
Inputs may be any that keep to these rules, and one draw needn't show every extreme that they name: `stick_map`: the 4096 values are distinct.
All inputs are finite; a program needn't handle non-finite values.
Results may differ from the reference program's by a relative error of at most 0.00007.
Values sent between devices are 32-bit elements; how exact they have to be, the bound alone decides.
No kernel may reach another device: no remote copies, remote signals or barrier semaphores. Data moves between devices by JAX's collectives and lax.ppermute only.
A program may use at most 64 MiB of HBM per device.

```python
import jax
import jax.numpy as jnp
from jax import lax

NG = 320
KZ = 128
STICKS = 4096
NB = 8


def draw_stick_map(key, part):
    key = jax.random.fold_in(key, 11)
    first_key, second_key = jax.random.split(key)
    inner = 1 + jax.random.permutation(first_key, KZ * KZ - 2)[:STICKS - 2]
    ends = jnp.array([0, KZ * KZ - 1], dtype=jnp.int32)
    whole = jnp.concatenate([ends, inner.astype(jnp.int32)])
    shuffle = jax.random.permutation(second_key, STICKS)
    return whole[shuffle]


def level_of(own_key, dims, shards, low, largest):
    def one(axis_at, parts):
        steps = jax.random.uniform(jax.random.fold_in(jax.random.fold_in(own_key, 6), axis_at), (parts,), jnp.float32, low / len(shards), largest / len(shards))
        return jnp.repeat(jnp.exp(steps), dims[axis_at] // parts).reshape((-1,) + (1,) * (len(dims) - axis_at - 1))

    factor_of = one(*shards[0])
    for cut in shards[1:]:
        factor_of = factor_of * one(*cut)
    return factor_of


def gaussian(rng, dims, width, reach, cuts=(), kind=jnp.bfloat16):
    loudness = level_of(rng, dims, cuts, -0.22, 0.18) if cuts else 1.0
    entries = jax.random.normal(rng, dims, jnp.float32) * width * loudness
    return jnp.minimum(jnp.maximum(entries, -reach), reach).astype(kind)


def setup_inputs(seed: int = 0) -> dict:
    key_list = jax.random.split(jax.random.key(seed), 7)
    orbitals = gaussian(key_list[0], (NB, STICKS, 2 * KZ), 1.0, 6.0, ((0, 4), (1, 64)), jnp.float32)
    applied_orbitals = gaussian(key_list[1], (NB, STICKS, 2 * KZ), 1.0, 6.0, ((0, 4), (1, 64)), jnp.float32)
    potential = gaussian(key_list[2], (NG, NG, NG), 1.0, 6.0, ((0, 64),), jnp.float32)
    stick_map = draw_stick_map(jax.random.fold_in(key_list[6], 71), 0)
    ritz_values = jnp.clip(jax.random.uniform(key_list[4], (NB,), jnp.float32, -1.0, 1.0) * level_of(key_list[4], (NB,), ((0, 4),), -0.4, 0.0), -1.0, 1.0)
    ritz_rotation = gaussian(key_list[5], (2 * NB, NB), (2 * NB) ** -0.5, 1.5, (), jnp.float32)
    return dict(orbitals=orbitals, applied_orbitals=applied_orbitals, potential=potential, stick_map=stick_map, ritz_values=ritz_values, ritz_rotation=ritz_rotation)


exact_mode = lax.Precision.HIGHEST


def stick_frequencies(stick_map):
    midpoint = KZ // 2
    across = stick_map // KZ - midpoint
    second = stick_map % KZ - midpoint
    vertical = jnp.arange(KZ, dtype=jnp.int32) - midpoint
    return across, second, vertical


def reference(orbitals, applied_orbitals, potential, stick_map, ritz_values, ritz_rotation):
    across, second, vertical = stick_frequencies(stick_map)
    midpoint = KZ // 2
    planar = (across * across + second * second).astype(jnp.float32)
    kinetic = (planar[:, None] + (vertical * vertical).astype(jnp.float32)[None, :]) / float(midpoint * midpoint)
    kinetic_both = jnp.concatenate([kinetic, kinetic], axis=1)
    correction = (applied_orbitals - ritz_values[:, None, None] * orbitals) / (1.0 + kinetic_both)
    index_x = (across % NG)[:, None]
    index_y = (second % NG)[:, None]
    index_z = (vertical % NG)[None, :]

    def apply_local(coefficients):
        values = lax.complex(coefficients[:, :KZ], coefficients[:, KZ:])
        grid_values = jnp.zeros((NG, NG, NG), values.dtype).at[index_z, index_x, index_y].set(values)
        real_field = jnp.fft.ifftn(grid_values, norm="ortho")
        spectrum = jnp.fft.fftn(potential * real_field, norm="ortho")
        picked = spectrum[index_z, index_x, index_y]
        return jnp.concatenate([jnp.real(picked), jnp.imag(picked)], axis=1)

    local_term = lax.map(apply_local, correction)
    applied_correction = kinetic_both * correction + local_term
    next_orbitals = jnp.einsum("bsk,bj->jsk", orbitals, ritz_rotation[:NB], precision=exact_mode)
    next_orbitals = next_orbitals + jnp.einsum("bsk,bj->jsk", correction, ritz_rotation[NB:], precision=exact_mode)
    return next_orbitals, applied_correction
```

```python
import functools
import math

import jax
import jax.numpy as jnp
import ml_dtypes
import numpy as np
from jax import lax
from jax.experimental import pallas as pl
from jax.experimental.pallas import tpu as pltpu
from jax.sharding import PartitionSpec as P

F32 = jnp.float32
BF16 = jnp.bfloat16
VMEM = pl.BlockSpec(memory_space=pltpu.VMEM)
SMEM = pl.BlockSpec(memory_space=pltpu.SMEM)
PARAMS = pltpu.CompilerParams(vmem_limit_bytes=56 * 1024 * 1024)

LENGTH = 320
WIDTH = 128
FINE = 2 * WIDTH
GROUP = 64
PLANES = LENGTH // GROUP
PARTS = 2 * PLANES
STICKS = GROUP * 64
BANDS = 2


def split_host(table):
    high = table.astype(ml_dtypes.bfloat16)
    low = (table - high.astype(np.float64)).astype(ml_dtypes.bfloat16)
    return high, low


def complex_table(length):
    frequencies = np.arange(WIDTH) - WIDTH // 2
    angles = 2.0 * math.pi * (np.outer(frequencies, np.arange(length)) % length) / length
    cosine, sine = np.cos(angles) / math.sqrt(length), np.sin(angles) / math.sqrt(length)
    return np.concatenate(
        [np.concatenate([cosine, sine], 1), np.concatenate([-sine, cosine], 1)], 0
    )


def resampling_table():
    places = np.arange(FINE)[:, None] * LENGTH - np.arange(LENGTH)[None, :] * FINE
    total = np.zeros((FINE, LENGTH))
    for d in range(-(WIDTH - 1), WIDTH):
        total += np.cos(2.0 * math.pi * ((places * d) % (FINE * LENGTH)) / (FINE * LENGTH))
    return total / LENGTH


def tables():
    square = complex_table(FINE)
    high, low = split_host(square)
    stick = complex_table(LENGTH).reshape(2 * WIDTH, 2, GROUP, PLANES)
    stick = stick.transpose(0, 2, 1, 3).reshape(2 * WIDTH, GROUP * PARTS)
    s_high, s_low = split_host(stick)
    r_high, r_low = split_host(resampling_table())
    three = np.concatenate
    return dict(
        row_up=three([high, high, low], 0),
        row_down=three([high.T, high.T, low.T], 0),
        col_up=three([high.T, low.T, high.T], 1),
        col_down=three([high, low, high], 1),
        stick_up=three([s_high.T, s_low.T, s_high.T], 1),
        stick_down=three([s_high, s_low, s_high], 1),
        fine_cols=three([r_high, r_low, r_high], 1),
        fine_rows=np.stack([r_high.T, r_low.T]),
    )


def halves(x):
    high = x.astype(BF16)
    low = (x - high.astype(F32)).astype(BF16)
    return high, low


def data_rows(x, axis):
    high, low = halves(x)
    return jnp.concatenate([high, high, low] if axis == 0 else [high, low, high], axis)


def dot(a, b):
    return jnp.dot(a, b, preferred_element_type=F32)


def planar_of(map_ref, sticks):
    me = lax.axis_index("pw")
    per_row = 128 // sticks
    row = map_ref[pl.ds(me // per_row, 1), :]
    fx = (row >> 7) - WIDTH // 2
    fy = (row & (WIDTH - 1)) - WIDTH // 2
    planar = (fx * fx + fy * fy).astype(F32)
    turned = jnp.broadcast_to(planar, (128, 128)).T
    upper = lax.rem(me, per_row) == 1
    return jnp.where(upper, turned[sticks:], turned[:sticks])


def kinetic_of(map_ref, sticks):
    planar = planar_of(map_ref, sticks)
    fz = lax.broadcasted_iota(jnp.int32, (1, WIDTH), 1) - WIDTH // 2
    return (planar + (fz * fz).astype(F32)) * (1.0 / (WIDTH // 2) ** 2)


def before_kernel(values_ref, rotation_ref, map_ref, orb_ref, app_ref, up_ref, send_ref, corr_ref, mix_ref):
    sticks = orb_ref.shape[1]
    kinetic = kinetic_of(map_ref, sticks)
    scale = 1.0 + jnp.concatenate([kinetic, kinetic], 1)
    corr = []
    for b in range(BANDS):
        c = (app_ref[b] - values_ref[b] * orb_ref[b]) / scale
        corr_ref[b] = c
        corr.append(c)
    rows = jnp.concatenate(corr, 0)
    turned = jnp.concatenate([rows[:, :128].T, rows[:, 128:].T], 0)
    send_ref[...] = dot(up_ref[...], data_rows(turned, 0))
    first = lax.axis_index("bg") * BANDS
    all_bands = mix_ref.shape[0]
    for j in range(all_bands):
        total = None
        for b in range(BANDS):
            term = rotation_ref[first + b, j] * orb_ref[b]
            term = term + rotation_ref[all_bands + first + b, j] * corr[b]
            total = term if total is None else total + term
        mix_ref[j] = total


def potential_kernel(pot_ref, rows_ref, cols_ref, out_ref, work):
    rows_high, rows_low = rows_ref[0], rows_ref[1]
    for p in range(PLANES):
        high, low = halves(pot_ref[p])
        part = dot(high, rows_high) + (dot(low, rows_high) + dot(high, rows_low))
        work[...] = data_rows(part, 0)
        out_ref[p] = dot(cols_ref[...], work[...])


def middle_kernel(
    place_ref, recv_ref, pot_ref, row_up, col_up, col_down, row_down, send_ref,
    sticks_ref, square_ref, turned_ref, rows_ref, half_ref, back_ref, out_ref,
):
    lane = lax.broadcasted_iota(jnp.int32, (1, 128), 1)
    lane_block = lane >> 5
    second_band = ((lane >> 4) & 1) == 1

    def unpack(d, _):
        real = recv_ref[pl.ds(d * PARTS, 8), :]
        imag = recv_ref[pl.ds(d * PARTS + 2, 8), :]
        turned = jnp.concatenate([real, imag] * 8, 0).T
        sticks_ref[pl.ds(pl.multiple_of(d * 64, 64), 64), :] = jnp.where(second_band, turned[64:], turned[:64])
        return 0

    lax.fori_loop(0, GROUP, unpack, 0, unroll=4)
    square_ref[...] = jnp.zeros_like(square_ref)

    def scatter(i, _):
        for j in range(16):
            s = i * 16 + j
            place = place_ref[s]
            pltpu.store(
                square_ref.at[pl.ds(place >> 2, 1), :],
                sticks_ref[pl.ds(s, 1), :],
                mask=lane_block == (place & 3),
            )
        return 0

    lax.fori_loop(0, STICKS // 16, scatter, 0)

    def turn(i, _):
        rows = pl.ds(pl.multiple_of(i * 128, 128), 128)
        turned_ref[rows, :] = square_ref[rows, :].T
        return 0

    lax.fori_loop(0, 32, turn, 0, unroll=4)
    for b in range(BANDS):
        for p in range(PLANES):
            at = (b * PLANES + p) * 128
            real = turned_ref[pl.ds(b * 16 + p, 128, stride=32), :]
            imag = turned_ref[pl.ds(b * 16 + 8 + 3 + p, 128, stride=32), :]
            rows_ref[at : at + 128, : 6 * 128] = data_rows(jnp.concatenate([real, imag], 1), 1)
    half_ref[...] = dot(rows_ref[:, : 6 * 128], row_up[...])
    for b in range(BANDS):
        for p in range(PLANES):
            at = (b * PLANES + p) * 128
            part = half_ref[at : at + 128, :]
            part = jnp.concatenate([part[:, :FINE], part[:, FINE:]], 0)
            field = dot(col_up[...], data_rows(part, 0))
            local = pot_ref[p]
            product = field * jnp.concatenate([local, local], 0)
            part = dot(col_down[...], data_rows(product, 0))
            part = jnp.concatenate([part[:128], part[128:]], 1)
            rows_ref[at : at + 128, :] = data_rows(part, 1)
    back_ref[...] = dot(rows_ref[...], row_down[...])
    for b in range(BANDS):
        for p in range(PLANES):
            at = (b * PLANES + p) * 128
            for c in range(2):
                turned_ref[pl.ds(b * 16 + c * 8 + p, 128, stride=32), :] = back_ref[
                    at : at + 128, c * 128 : c * 128 + 128
                ]

    def turn_back(i, _):
        rows = pl.ds(pl.multiple_of(i * 128, 128), 128)
        square_ref[rows, :] = turned_ref[rows, :].T
        return 0

    lax.fori_loop(0, 32, turn_back, 0, unroll=4)

    def gather(i, _):
        for j in range(16):
            s = i * 16 + j
            place = place_ref[s]
            row = square_ref[pl.ds(place >> 2, 1), :]
            sticks_ref[pl.ds(s, 1), :] = jnp.where(lane_block == (place & 3), row, 0.0)
        return 0

    lax.fori_loop(0, STICKS // 16, gather, 0)

    def pack(d, _):
        rows = sticks_ref[pl.ds(pl.multiple_of(d * 64, 64), 64), :]
        upper = jnp.where(second_band, 0.0, rows)
        lower = jnp.where(second_band, rows, 0.0)
        turned = jnp.concatenate([upper, lower], 0).T
        total = turned[:16]
        for k in range(1, 8):
            total = total + turned[16 * k : 16 * k + 16]
        out_ref[pl.ds(d * PARTS, PLANES), :] = total[:PLANES]
        out_ref[pl.ds(d * PARTS + PLANES, PLANES), :] = total[8 : 8 + PLANES]
        return 0

    lax.fori_loop(0, GROUP, pack, 0, unroll=4)
    send_ref[...] = out_ref[...]


def after_kernel(map_ref, corr_ref, recv_ref, down_ref, out_ref):
    sticks = corr_ref.shape[1]
    kinetic = kinetic_of(map_ref, sticks)
    local = dot(down_ref[...], data_rows(recv_ref[...], 0))
    local = jnp.concatenate([local[:128].T, local[128:].T], 1)
    both = jnp.concatenate([kinetic, kinetic], 1)
    for b in range(BANDS):
        out_ref[b] = both * corr_ref[b] + local[b * sticks : (b + 1) * sticks]


def shape(*dims):
    return jax.ShapeDtypeStruct(dims, F32)


def exchange(values):
    values = values.reshape(GROUP, 1, PARTS * 128)
    return lax.all_to_all(values, "pw", 0, 0, tiled=True).reshape(GROUP * PARTS, 128)


def middle(place, received, local, t):
    return pl.pallas_call(
        middle_kernel,
        out_shape=shape(GROUP * PARTS, 128),
        in_specs=[SMEM] + [VMEM] * 6,
        out_specs=VMEM,
        scratch_shapes=[
            pltpu.VMEM((STICKS, 128), F32),
            pltpu.VMEM((STICKS, 128), F32),
            pltpu.VMEM((STICKS, 128), F32),
            pltpu.VMEM((BANDS * PLANES * 128, 6 * FINE), BF16),
            pltpu.VMEM((BANDS * PLANES * 128, 2 * FINE), F32),
            pltpu.VMEM((BANDS * PLANES * 128, FINE), F32),
            pltpu.VMEM((GROUP * PARTS, 128), F32),
        ],
        compiler_params=PARAMS,
        name="middle",
    )(place, received, local, t["row_up"], t["col_up"], t["col_down"], t["row_down"])


def fine_potential(potential, t):
    return pl.pallas_call(
        potential_kernel,
        out_shape=shape(PLANES, FINE, FINE),
        in_specs=[VMEM] * 3,
        out_specs=VMEM,
        scratch_shapes=[pltpu.VMEM((3 * LENGTH, FINE), BF16)],
        compiler_params=PARAMS,
        name="fine_potential",
    )(potential, t["fine_rows"], t["fine_cols"])


def on_device(orbitals, applied_orbitals, potential, stick_map, ritz_values, ritz_rotation):
    t = {name: jnp.asarray(value) for name, value in tables().items()}
    sticks = orbitals.shape[1]
    all_bands = ritz_rotation.shape[1]
    map_rows = stick_map.reshape(-1, 128)
    place = ((stick_map >> 9) << 9) | ((stick_map & 127) << 2) | ((stick_map >> 7) & 3)
    sent, correction, mixed = pl.pallas_call(
        before_kernel,
        out_shape=(shape(GROUP * PARTS, 128), shape(*orbitals.shape), shape(all_bands, sticks, 2 * WIDTH)),
        in_specs=[SMEM, SMEM] + [VMEM] * 4,
        out_specs=(VMEM, VMEM, VMEM),
        compiler_params=PARAMS,
        name="before",
    )(ritz_values, ritz_rotation, map_rows, orbitals, applied_orbitals, t["stick_up"])
    local = fine_potential(potential, t)
    next_orbitals = lax.psum_scatter(mixed, "bg", scatter_dimension=0, tiled=True)
    received = exchange(sent)
    returned = exchange(middle(place, received, local, t))
    applied_correction = pl.pallas_call(
        after_kernel,
        out_shape=shape(*orbitals.shape),
        in_specs=[VMEM] * 4,
        out_specs=VMEM,
        compiler_params=PARAMS,
        name="after",
    )(map_rows, correction, returned, t["stick_down"])
    return (next_orbitals, applied_correction)


def solution(mesh):
    return jax.shard_map(
        on_device,
        mesh=mesh,
        in_specs=(P("bg", "pw", None), P("bg", "pw", None), P("pw", None, None), P(), P("bg"), P()),
        out_specs=(P("bg", "pw", None), P("bg", "pw", None)),
        check_vma=False,
    )
```

```python
import functools
import math

import jax
import jax.numpy as jnp
import ml_dtypes
import numpy as np
from jax import lax
from jax.experimental import pallas as pl
from jax.experimental.pallas import tpu as pltpu
from jax.sharding import PartitionSpec as P

F32 = jnp.float32
BF16 = jnp.bfloat16
VMEM = pl.BlockSpec(memory_space=pltpu.VMEM)
SMEM = pl.BlockSpec(memory_space=pltpu.SMEM)
ANY = pl.BlockSpec(memory_space=pl.ANY)
PARAMS = pltpu.CompilerParams(vmem_limit_bytes=40 * 1024 * 1024)

LENGTH = 320
WIDTH = 128
FINE = 2 * WIDTH
GROUP = 64
PLANES = LENGTH // GROUP
PARTS = 2 * PLANES
STICKS = GROUP * 64
BANDS = 2


def split_host(table):
    high = table.astype(ml_dtypes.bfloat16)
    low = (table - high.astype(np.float64)).astype(ml_dtypes.bfloat16)
    return high, low


def complex_table(length):
    frequencies = np.arange(WIDTH) - WIDTH // 2
    angles = 2.0 * math.pi * (np.outer(frequencies, np.arange(length)) % length) / length
    cosine, sine = np.cos(angles) / math.sqrt(length), np.sin(angles) / math.sqrt(length)
    return np.concatenate(
        [np.concatenate([cosine, sine], 1), np.concatenate([-sine, cosine], 1)], 0
    )


def resampling_table():
    places = np.arange(FINE)[:, None] * LENGTH - np.arange(LENGTH)[None, :] * FINE
    total = np.zeros((FINE, LENGTH))
    for d in range(-(WIDTH - 1), WIDTH):
        total += np.cos(2.0 * math.pi * ((places * d) % (FINE * LENGTH)) / (FINE * LENGTH))
    return total / LENGTH


def spreading_table():
    table = np.zeros((2, 2, 8, 16, 8, 4, 2, 16))
    for b in range(2):
        for k in range(8):
            for part in range(16):
                table[b, :, k, part, k, :, b, part] = 1.0
    return table.reshape(512, 1024).astype(ml_dtypes.bfloat16)


def choosing_table():
    table = np.zeros((2, 16, 2, 4, 2, 16))
    for b in range(2):
        for part in range(16):
            table[b, part, :, :, b, part] = 1.0
    return table.reshape(32, 256).astype(ml_dtypes.bfloat16)


def tables():
    square = complex_table(FINE)
    high, low = split_host(square)
    stick = complex_table(LENGTH).reshape(2 * WIDTH, 2, GROUP, PLANES)
    stick = stick.transpose(0, 2, 1, 3).reshape(2 * WIDTH, GROUP * PARTS)
    s_high, s_low = split_host(stick)
    r_high, r_low = split_host(resampling_table())
    three = np.concatenate
    return dict(
        row_up=three([high, high, low], 0),
        row_down=three([high.T, high.T, low.T], 0),
        col_up=three([high.T, low.T, high.T], 1),
        col_down=three([high, low, high], 1),
        stick_up=three([s_high.T, s_low.T, s_high.T], 1),
        stick_down=three([s_high, s_low, s_high], 1),
        fine_cols=three([r_high, r_low, r_high], 1),
        spread=spreading_table(),
        choose=choosing_table(),
        fine_rows=np.stack([r_high.T, r_low.T]),
    )


def halves(x):
    high = x.astype(BF16)
    low = (x - high.astype(F32)).astype(BF16)
    return high, low


def data_rows(x, axis):
    high, low = halves(x)
    return jnp.concatenate([high, high, low] if axis == 0 else [high, low, high], axis)


def dot(a, b):
    return jnp.dot(a, b, preferred_element_type=F32)


def planar_of(map_ref, sticks):
    me = lax.axis_index("pw")
    per_row = 128 // sticks
    row = map_ref[pl.ds(me // per_row, 1), :]
    fx = (row >> 7) - WIDTH // 2
    fy = (row & (WIDTH - 1)) - WIDTH // 2
    planar = (fx * fx + fy * fy).astype(F32)
    turned = jnp.broadcast_to(planar, (128, 128)).T
    upper = lax.rem(me, per_row) == 1
    return jnp.where(upper, turned[sticks:], turned[:sticks])


def kinetic_of(map_ref, sticks):
    planar = planar_of(map_ref, sticks)
    fz = lax.broadcasted_iota(jnp.int32, (1, WIDTH), 1) - WIDTH // 2
    return (planar + (fz * fz).astype(F32)) * (1.0 / (WIDTH // 2) ** 2)


def before_kernel(values_ref, map_ref, orb_ref, app_ref, up_ref, send_ref, corr_ref):
    sticks = orb_ref.shape[1]
    kinetic = kinetic_of(map_ref, sticks)
    scale = 1.0 + jnp.concatenate([kinetic, kinetic], 1)
    corr = []
    for b in range(BANDS):
        c = (app_ref[b] - values_ref[b] * orb_ref[b]) / scale
        corr_ref[b] = c
        corr.append(c)
    rows = jnp.concatenate(corr, 0)
    turned = jnp.concatenate([rows[:, :128].T, rows[:, 128:].T], 0)
    send_ref[...] = dot(up_ref[...], data_rows(turned, 0))


def prepare_kernel(
    rotation_ref, map_ref, orb_ref, corr_ref, pot_hbm, rows_ref, cols_ref, out_ref, mask_ref, place_ref, keep_ref, pass_ref,
    pot_ref, work_ref, sems,
):
    copies = []
    for p in range(PLANES):
        copies.append(pltpu.make_async_copy(pot_hbm.at[p], pot_ref.at[p], sems.at[p]))
        copies[-1].start()
    me = lax.axis_index("bg")
    all_bands = rotation_ref.shape[0]
    for target, group in ((keep_ref, me), (pass_ref, me ^ 1)):
        for k, owner in enumerate((group, 3 - group)):
            for i in range(BANDS):
                j = owner * BANDS + i
                total = None
                for b in range(BANDS):
                    term = rotation_ref[j, me * BANDS + b] * orb_ref[b]
                    term = term + rotation_ref[j, all_bands + me * BANDS + b] * corr_ref[b]
                    total = term if total is None else total + term
                target[k, i] = total
    place_ref[...] = ((map_ref[...] >> 9) << 7) | (map_ref[...] & 127)
    lane_block = lax.broadcasted_iota(jnp.int32, (128, 128), 1) >> 5

    def mark(i, _):
        blocks = jnp.broadcast_to((map_ref[pl.ds(i, 1), :] >> 7) & 3, (128, 128)).T
        mask_ref[pl.ds(pl.multiple_of(i * 128, 128), 128), :] = jnp.where(blocks == lane_block, 1.0, 0.0)
        return 0

    lax.fori_loop(0, STICKS // 128, mark, 0, unroll=4)
    rows_high, rows_low = rows_ref[0], rows_ref[1]
    for p in range(PLANES):
        copies[p].wait()
        for at in range(0, LENGTH, LENGTH // 2):
            high, low = halves(pot_ref[p, at : at + LENGTH // 2, :])
            part = dot(high, rows_high) + (dot(low, rows_high) + dot(high, rows_low))
            high, low = halves(part)
            work_ref[p, at : at + LENGTH // 2] = high
            work_ref[p, LENGTH + at : LENGTH + at + LENGTH // 2] = high
            work_ref[p, 2 * LENGTH + at : 2 * LENGTH + at + LENGTH // 2] = low
        out_ref[p] = dot(cols_ref[...], work_ref[p])


def middle_kernel(
    place_hbm, recv_ref, pot_hbm, mask_ref, spread_hbm, row_up_hbm, col_up_hbm, col_down_hbm, row_down_hbm, choose_hbm,
    send_ref,
    place_ref, pot_ref, sticks_ref, square_ref, turned_ref, rows_ref, half_ref, back_ref,
    spread, row_up, col_up, col_down, row_down, choose, sems,
):
    copies = [
        pltpu.make_async_copy(source, target, sems.at[i])
        for i, (source, target) in enumerate(
            (
                (spread_hbm, spread),
                (place_hbm, place_ref),
                (row_up_hbm, row_up),
                (pot_hbm, pot_ref),
                (col_up_hbm, col_up),
                (col_down_hbm, col_down),
                (row_down_hbm, row_down),
                (choose_hbm, choose),
            )
        )
    ]
    for copy in copies:
        copy.start()
    square_ref[...] = jnp.zeros_like(square_ref)
    lane = lax.broadcasted_iota(jnp.int32, (1, 128), 1)

    for g in range(GROUP // 8):
        parts = []
        for d in range(8 * g, 8 * g + 8):
            parts += [recv_ref[d * PARTS : d * PARTS + 8, :], recv_ref[d * PARTS + 2 : d * PARTS + 10, :]]
        turned = jnp.concatenate(parts, 0).T
        first, second = halves(turned[:64]), halves(turned[64:])
        rows_ref[g * 64 : g * 64 + 64, :512] = jnp.concatenate([*first, *second], 1)
    copies[0].wait()
    for g in range(0, GROUP // 8, 4):
        found = dot(rows_ref[g * 64 : g * 64 + 256, :512], spread[...])
        for h in range(4):
            for k in range(8):
                at = (8 * (g + h) + k) * 64
                sticks_ref[at : at + 64, :] = found[h * 64 : h * 64 + 64, k * 128 : k * 128 + 128]
    copies[1].wait()

    def scatter(i, _):
        first = pl.multiple_of(i * 128, 128)
        for j in range(128):
            pltpu.store(
                square_ref.at[pl.ds(place_ref[i, j], 1), :],
                sticks_ref[pl.ds(first + j, 1), :],
                mask=mask_ref[pl.ds(first + j, 1), :] != 0.0,
            )
        return 0

    lax.fori_loop(0, STICKS // 128, scatter, 0)

    def turn(i, _):
        rows = pl.ds(pl.multiple_of(i * 128, 128), 128)
        turned_ref[rows, :] = square_ref[rows, :].T
        return 0

    lax.fori_loop(0, 32, turn, 0, unroll=4)
    pairs = [(b, p) for b in range(BANDS) for p in range(PLANES)]
    copies[2].wait()
    for k, (b, p) in enumerate(pairs):
        real = turned_ref[pl.ds(b * 16 + p, 128, stride=32), :]
        imag = turned_ref[pl.ds(b * 16 + 8 + 3 + p, 128, stride=32), :]
        rows_ref[k * 128 : k * 128 + 128, : 6 * 128] = data_rows(jnp.concatenate([real, imag], 1), 1)
        if k % 2 == 1:
            at = (k - 1) * 128
            half_ref[at : at + 256, :] = dot(rows_ref[at : at + 256, : 6 * 128], row_up[...])
    for copy in copies[3:]:
        copy.wait()
    for k, (b, p) in enumerate(pairs):
        part = half_ref[k * 128 : k * 128 + 128, :]
        part = jnp.concatenate([part[:, :FINE], part[:, FINE:]], 0)
        field = dot(col_up[...], data_rows(part, 0))
        local = pot_ref[p]
        product = field * jnp.concatenate([local, local], 0)
        part = dot(col_down[...], data_rows(product, 0))
        part = jnp.concatenate([part[:128], part[128:]], 1)
        rows_ref[k * 128 : k * 128 + 128, :] = data_rows(part, 1)
        if k % 2 == 1:
            at = (k - 1) * 128
            back_ref[at : at + 256, :] = dot(rows_ref[at : at + 256, :], row_down[...])
    for k, (b, p) in enumerate(pairs):
        for c in range(2):
            turned_ref[pl.ds(b * 16 + c * 8 + p, 128, stride=32), :] = back_ref[
                k * 128 : k * 128 + 128, c * 128 : c * 128 + 128
            ]

    def turn_back(i, _):
        rows = pl.ds(pl.multiple_of(i * 128, 128), 128)
        square_ref[rows, :] = turned_ref[rows, :].T
        return 0

    lax.fori_loop(0, 32, turn_back, 0, unroll=4)

    def gather(i, _):
        first = pl.multiple_of(i * 128, 128)
        for j in range(128):
            sticks_ref[pl.ds(first + j, 1), :] = square_ref[pl.ds(place_ref[i, j], 1), :]
        return 0

    lax.fori_loop(0, STICKS // 128, gather, 0)
    left = lane < 64
    for at in range(0, STICKS, 256):
        rows = jnp.where(mask_ref[at : at + 256, :] != 0.0, sticks_ref[at : at + 256, :], 0.0)
        found = lax.dot_general(
            choose[...],
            jnp.concatenate(halves(rows), 1),
            (((1,), (1,)), ((), ())),
            preferred_element_type=F32,
        )
        for h in range(2):
            here = found[:, h * 128 : h * 128 + 128]
            swapped = pltpu.roll(here, 64, 1)
            for i, part in enumerate(
                (jnp.where(left, here[:16], swapped[16:]), jnp.where(left, swapped[:16], here[16:]))
            ):
                to = (at // 64 + 2 * h + i) * PARTS
                send_ref[to : to + PLANES, :] = part[:PLANES]
                send_ref[to + PLANES : to + PARTS, :] = part[8 : 8 + PLANES]


def after_kernel(map_ref, corr_ref, recv_ref, down_ref, half_ref, last_ref, out_ref, next_ref):
    sticks = corr_ref.shape[1]
    kinetic = kinetic_of(map_ref, sticks)
    local = dot(down_ref[...], data_rows(recv_ref[...], 0))
    local = jnp.concatenate([local[:128].T, local[128:].T], 1)
    both = jnp.concatenate([kinetic, kinetic], 1)
    for b in range(BANDS):
        out_ref[b] = both * corr_ref[b] + local[b * sticks : (b + 1) * sticks]
        next_ref[b] = half_ref[b] + last_ref[b]


def shape(*dims):
    return jax.ShapeDtypeStruct(dims, F32)


def exchange(values):
    values = values.reshape(GROUP, 1, PARTS * 128)
    return lax.all_to_all(values, "pw", 0, 0, tiled=True).reshape(GROUP * PARTS, 128)


def in_vmem(x):
    return pltpu.with_memory_space_constraint(x, pltpu.VMEM)


def in_hbm(x):
    return pltpu.with_memory_space_constraint(x, pltpu.HBM)


def cost(us):
    return pl.CostEstimate(flops=int(us * 1e9), bytes_accessed=int(us * 3e6), transcendentals=0)


def call(kernel, name, us, inputs, out_shape, in_specs, out_specs, scratch=()):
    return pl.pallas_call(
        kernel,
        out_shape=out_shape,
        in_specs=in_specs,
        out_specs=out_specs,
        scratch_shapes=list(scratch),
        compiler_params=PARAMS,
        cost_estimate=cost(us),
        name=name,
    )(*inputs)


def middle(place, received, local, mask, t):
    grid = BANDS * PLANES * 128
    names = ("spread", "row_up", "col_up", "col_down", "row_down", "choose")
    return call(
        middle_kernel,
        "middle",
        20,
        (in_hbm(place), in_vmem(received), in_hbm(local), in_vmem(mask), *(in_hbm(t[n]) for n in names)),
        shape(GROUP * PARTS, 128),
        [ANY, VMEM, ANY, VMEM] + [ANY] * 6,
        VMEM,
        [
            pltpu.SMEM((STICKS // 128, 128), jnp.int32),
            pltpu.VMEM((PLANES, FINE, FINE), F32),
            pltpu.VMEM((STICKS, 128), F32),
            pltpu.VMEM((STICKS, 128), F32),
            pltpu.VMEM((STICKS, 128), F32),
            pltpu.VMEM((grid, 6 * FINE), BF16),
            pltpu.VMEM((grid, 2 * FINE), F32),
            pltpu.VMEM((grid, FINE), F32),
            *(pltpu.VMEM(t[n].shape, BF16) for n in names),
            pltpu.SemaphoreType.DMA((8,)),
        ],
    )


def prepare(rotation, map_rows, orbitals, correction, potential, t):
    bands, sticks, doubled = orbitals.shape
    return call(
        prepare_kernel,
        "prepare",
        7,
        tuple(
            in_hbm(x)
            for x in (rotation, map_rows, orbitals, correction, potential, t["fine_rows"], t["fine_cols"])
        ),
        (
            pltpu.HBM((PLANES, FINE, FINE), F32),
            pltpu.VMEM((STICKS, 128), F32),
            pltpu.HBM(map_rows.shape, jnp.int32),
            pltpu.HBM((2, BANDS, sticks, doubled), F32),
            pltpu.HBM((2, BANDS, sticks, doubled), F32),
        ),
        [SMEM] + [VMEM] * 3 + [ANY] + [VMEM] * 2,
        (VMEM,) * 5,
        [
            pltpu.VMEM((PLANES, LENGTH, LENGTH), F32),
            pltpu.VMEM((PLANES, 3 * LENGTH, FINE), BF16),
            pltpu.SemaphoreType.DMA((PLANES,)),
        ],
    )


def on_device(orbitals, applied_orbitals, potential, stick_map, ritz_values, ritz_rotation):
    t = {name: jnp.asarray(value) for name, value in tables().items()}
    map_rows = stick_map.reshape(-1, 128)
    sent, correction = call(
        before_kernel,
        "before",
        2,
        tuple(in_hbm(x) for x in (ritz_values, map_rows, orbitals, applied_orbitals, t["stick_up"])),
        (pltpu.HBM((GROUP * PARTS, 128), F32), pltpu.HBM(orbitals.shape, F32)),
        [SMEM] + [VMEM] * 4,
        (VMEM, VMEM),
    )
    received = exchange(sent)
    local, mask, place, kept, passed = prepare(ritz_rotation.T, map_rows, orbitals, correction, potential, t)
    came = lax.ppermute(passed, "bg", [(i, i ^ 1) for i in range(4)])
    product, came = lax.optimization_barrier((middle(place, received, local, mask, t), came))
    returned = exchange(product)
    halved = kept + came
    last = lax.ppermute(halved[1], "bg", [(i, 3 - i) for i in range(4)])
    applied_correction, next_orbitals = call(
        after_kernel,
        "after",
        2,
        (in_hbm(map_rows), in_hbm(correction), in_vmem(returned), in_hbm(t["stick_down"]), halved[0], last),
        (shape(*orbitals.shape), shape(*orbitals.shape)),
        [VMEM] * 6,
        (VMEM, VMEM),
    )
    return (next_orbitals, applied_correction)


def solution(mesh):
    return jax.shard_map(
        on_device,
        mesh=mesh,
        in_specs=(P("bg", "pw", None), P("bg", "pw", None), P("pw", None, None), P(), P("bg"), P()),
        out_specs=(P("bg", "pw", None), P("bg", "pw", None)),
        check_vma=False,
    )
```

```python
import functools
import math

import jax
import jax.numpy as jnp
import ml_dtypes
import numpy as np
from jax import lax
from jax.experimental import pallas as pl
from jax.experimental.pallas import tpu as pltpu
from jax.sharding import PartitionSpec as P

F32 = jnp.float32
BF16 = jnp.bfloat16
VMEM = pl.BlockSpec(memory_space=pltpu.VMEM)
SMEM = pl.BlockSpec(memory_space=pltpu.SMEM)
ANY = pl.BlockSpec(memory_space=pl.ANY)
PARAMS = pltpu.CompilerParams(vmem_limit_bytes=32 * 1024 * 1024)

LENGTH = 320
WIDTH = 128
FINE = 2 * WIDTH
GROUP = 64
PLANES = LENGTH // GROUP
PARTS = 2 * PLANES
STICKS = GROUP * 64
BANDS = 2


def split_host(table):
    high = table.astype(ml_dtypes.bfloat16)
    low = (table - high.astype(np.float64)).astype(ml_dtypes.bfloat16)
    return high, low


HALF = WIDTH // 2


def frequency_slots():
    return np.concatenate([np.arange(HALF), [-HALF], -np.arange(1, HALF)])


def point_slots():
    return np.concatenate([np.arange(WIDTH), [WIDTH], -np.arange(1, WIDTH)])


def complex_table(frequencies, points, length):
    angles = 2.0 * math.pi * (np.outer(frequencies, points) % length) / length
    cosine, sine = np.cos(angles) / math.sqrt(length), np.sin(angles) / math.sqrt(length)
    return np.concatenate(
        [np.concatenate([cosine, sine], 1), np.concatenate([-sine, cosine], 1)], 0
    )


def wave(function, frequencies, points):
    angles = 2.0 * math.pi * (np.outer(frequencies, points) % FINE) / FINE
    return function(angles) / math.sqrt(FINE)


def folded_tables():
    zeros = np.zeros
    pairs, near = np.arange(HALF), np.arange(WIDTH)
    three = np.concatenate

    def joined(main, single):
        high, low = split_host(main)
        return three([high, high, low, single.astype(ml_dtypes.bfloat16)], 1)

    points = point_slots()
    sines = -wave(np.sin, pairs, points)
    sines[0] = wave(np.sin, [HALF], points)
    single = zeros((FINE, WIDTH))
    single[:, 0] = single[:, HALF] = wave(np.cos, [HALF], points)[0]
    row_up = joined(three([wave(np.cos, pairs, points), sines], 0).T, single).T
    single = zeros((WIDTH + 16, 16))
    single[: WIDTH + 1, 0] = single[: WIDTH + 1, 8] = wave(np.cos, [HALF], np.arange(WIDTH + 1))[0]
    even = zeros((WIDTH + 16, HALF))
    even[: WIDTH + 1] = wave(np.cos, pairs, np.arange(WIDTH + 1)).T
    even_up = joined(even, single)
    single = zeros((WIDTH, 16))
    single[:, 0] = single[:, 8] = -wave(np.sin, [HALF], near)[0]
    odd_up = joined(wave(np.sin, pairs, near).T, single)
    single = zeros((HALF + 16, 16))
    single[: HALF + 1, 0] = single[: HALF + 1, 8] = wave(np.cos, np.arange(HALF + 1), [WIDTH])[:, 0]
    even = zeros((HALF + 16, WIDTH))
    even[: HALF + 1] = wave(np.cos, np.arange(HALF + 1), near)
    even_down = joined(even, single)
    odd_high, odd_low = split_host(wave(np.sin, [HALF, *range(1, HALF)], near))
    odd_down = three([odd_high, odd_high, odd_low], 1)
    return dict(row_up=row_up, even_up=even_up, odd_up=odd_up, even_down=even_down, odd_down=odd_down)


def resampling_table():
    places = point_slots()[:, None] * LENGTH - np.arange(LENGTH)[None, :] * FINE
    total = np.zeros((FINE, LENGTH))
    for d in range(-(WIDTH - 1), WIDTH):
        total += np.cos(2.0 * math.pi * ((places * d) % (FINE * LENGTH)) / (FINE * LENGTH))
    return total / LENGTH


def spreading_table():
    table = np.zeros((2, 2, 8, 16, 8, 4, 2, 16))
    for b in range(2):
        for k in range(8):
            for part in range(16):
                table[b, :, k, part, k, :, b, part] = 1.0
    return table.reshape(512, 1024).astype(ml_dtypes.bfloat16)


def choosing_table():
    table = np.zeros((2, 16, 2, 4, 2, 16))
    for b in range(2):
        for part in range(16):
            table[b, part, :, :, b, part] = 1.0
    return table.reshape(32, 256).astype(ml_dtypes.bfloat16)


def tables():
    high, low = split_host(complex_table(frequency_slots(), point_slots(), FINE))
    stick = complex_table(np.arange(WIDTH) - HALF, np.arange(LENGTH), LENGTH).reshape(2 * WIDTH, 2, GROUP, PLANES)
    stick = stick.transpose(0, 2, 1, 3).reshape(2 * WIDTH, GROUP * PARTS)
    s_high, s_low = split_host(stick)
    r_high, r_low = split_host(resampling_table())
    three = np.concatenate
    return dict(
        **folded_tables(),
        row_down=three([high.T, high.T, low.T], 0),
        stick_up=three([s_high.T, s_low.T, s_high.T], 1),
        stick_down=three([s_high, s_low, s_high], 1),
        fine_cols=three([r_high, r_low, r_high], 1),
        spread=spreading_table(),
        choose=choosing_table(),
        fine_rows=np.stack([r_high.T, r_low.T]),
    )


def halves(x):
    high = x.astype(BF16)
    low = (x - high.astype(F32)).astype(BF16)
    return high, low


def data_rows(x, axis):
    high, low = halves(x)
    return jnp.concatenate([high, high, low] if axis == 0 else [high, low, high], axis)


def dot(a, b):
    return jnp.dot(a, b, preferred_element_type=F32)


def slot_of(index):
    return jnp.where(index >= HALF, index - HALF, HALF + ((HALF - index) & (HALF - 1)))


def bare_first(x):
    first = lax.broadcasted_iota(jnp.int32, (8, 1), 0) == 0
    return jnp.concatenate([jnp.where(first, 0.0, x[:8]), x[8:]], 0)


def other_first(x, other):
    first = lax.broadcasted_iota(jnp.int32, (8, 1), 0) == 0
    return jnp.concatenate([jnp.where(first, other[:8], x[:8]), x[8:]], 0)


def folded_data(x, single=None):
    high, low = halves(x)
    parts = [high, low, high]
    if single is not None:
        top = single[:8]
        top_high = top.astype(BF16).astype(F32)
        parts.append(jnp.concatenate([top_high, top - top_high], 0).astype(BF16))
    return jnp.concatenate(parts, 0)


def planar_of(map_ref, sticks):
    me = lax.axis_index("pw")
    per_row = 128 // sticks
    row = map_ref[pl.ds(me // per_row, 1), :]
    fx = (row >> 7) - WIDTH // 2
    fy = (row & (WIDTH - 1)) - WIDTH // 2
    planar = (fx * fx + fy * fy).astype(F32)
    turned = jnp.broadcast_to(planar, (128, 128)).T
    upper = lax.rem(me, per_row) == 1
    return jnp.where(upper, turned[sticks:], turned[:sticks])


def kinetic_of(map_ref, sticks):
    planar = planar_of(map_ref, sticks)
    fz = lax.broadcasted_iota(jnp.int32, (1, WIDTH), 1) - WIDTH // 2
    return (planar + (fz * fz).astype(F32)) * (1.0 / (WIDTH // 2) ** 2)


def before_kernel(values_ref, map_ref, orb_ref, app_ref, up_ref, send_ref, corr_ref):
    sticks = orb_ref.shape[1]
    kinetic = kinetic_of(map_ref, sticks)
    scale = 1.0 + jnp.concatenate([kinetic, kinetic], 1)
    corr = []
    for b in range(BANDS):
        c = (app_ref[b] - values_ref[b] * orb_ref[b]) / scale
        corr_ref[b] = c
        corr.append(c)
    rows = jnp.concatenate(corr, 0)
    turned = jnp.concatenate([rows[:, :128].T, rows[:, 128:].T], 0)
    send_ref[...] = dot(up_ref[...], data_rows(turned, 0))


def prepare_kernel(
    rotation_ref, map_ref, orb_ref, corr_ref, pot_hbm, rows_ref, cols_ref, out_ref, bits_ref, place_ref, keep_ref, pass_ref,
    pot_ref, work_ref, sems,
):
    copies = [
        pltpu.make_async_copy(pot_hbm.at[p], pot_ref.at[pl.ds(p * LENGTH, LENGTH), :], sems.at[p]) for p in range(PLANES)
    ]
    for copy in copies:
        copy.start()
    me = lax.axis_index("bg")
    all_bands = rotation_ref.shape[0]
    for target, group in ((keep_ref, me), (pass_ref, me ^ 1)):
        for k, owner in enumerate((group, 3 - group)):
            for i in range(BANDS):
                j = owner * BANDS + i
                total = None
                for b in range(BANDS):
                    term = rotation_ref[j, me * BANDS + b] * orb_ref[b]
                    term = term + rotation_ref[j, all_bands + me * BANDS + b] * corr_ref[b]
                    total = term if total is None else total + term
                target[k, i] = total
    columns = slot_of(map_ref[...] >> 7)
    place_ref[...] = ((columns >> 2) << 7) | slot_of(map_ref[...] & 127)
    columns = columns & 3
    row_block = lax.broadcasted_iota(jnp.int32, (128, 128), 0) >> 5
    stick = lax.broadcasted_iota(jnp.int32, (16, 128), 1)
    eight = lax.broadcasted_iota(jnp.int32, (16, 128), 0)
    weights = jnp.where((stick >> 3) == eight, (1 << (stick & 7)).astype(F32), 0.0).astype(BF16)
    rows_high, rows_low = rows_ref[0], rows_ref[1]
    marked = arrived = done = 0
    for at in range(0, PLANES * LENGTH, 256):
        end = min(at + 256, PLANES * LENGTH)
        while arrived * LENGTH < end:
            copies[arrived].wait()
            arrived += 1
        high, low = halves(pot_ref[at:end, :])
        part = dot(high, rows_high) + (dot(low, rows_high) + dot(high, rows_low))
        high, low = halves(part)
        for p in range(at // LENGTH, (end - 1) // LENGTH + 1):
            first, stop = max(at, p * LENGTH), min(end, (p + 1) * LENGTH)
            for k, values in enumerate((high, high, low)):
                to = k * LENGTH + first - p * LENGTH
                work_ref[p, to : to + stop - first] = values[first - at : stop - at]
        while (done + 1) * LENGTH <= end:
            out_ref[done] = dot(cols_ref[...], work_ref[done])
            done += 1
        while marked < STICKS // 128 and marked < (at // 256 + 1) * 5:
            match = jnp.where(columns[marked : marked + 1, :] == row_block, 1.0, 0.0).astype(BF16)
            bits = lax.dot_general(weights, match, (((1,), (1,)), ((), ())), preferred_element_type=F32)
            bits_ref[marked * 16 : marked * 16 + 16, :] = bits.astype(jnp.int32)
            marked += 1


def middle_kernel(
    place_hbm, recv_ref, pot_ref, bits_ref, spread_hbm, row_up_hbm, even_up_hbm, odd_up_hbm, even_down_hbm,
    odd_down_hbm, row_down_hbm, choose_hbm,
    send_ref,
    place_ref, sticks_ref, square_ref, turned_ref, rows_ref, half_ref, back_ref,
    spread, row_up, even_up, odd_up, even_down, odd_down, row_down, choose, sems,
):
    copies = [
        pltpu.make_async_copy(source, target, sems.at[i])
        for i, (source, target) in enumerate(
            (
                (spread_hbm, spread),
                (place_hbm, place_ref),
                (row_up_hbm, row_up),
                (even_up_hbm, even_up),
                (odd_up_hbm, odd_up),
                (even_down_hbm, even_down),
                (odd_down_hbm, odd_down),
                (row_down_hbm, row_down),
                (choose_hbm, choose),
            )
        )
    ]
    for copy in copies:
        copy.start()
    square_ref[...] = jnp.zeros_like(square_ref)
    lane = lax.broadcasted_iota(jnp.int32, (1, 128), 1)

    for g in range(GROUP // 8):
        parts = []
        for d in range(8 * g, 8 * g + 8):
            parts += [recv_ref[d * PARTS : d * PARTS + 8, :], recv_ref[d * PARTS + 2 : d * PARTS + 10, :]]
        turned = jnp.concatenate(parts, 0).T
        first, second = halves(turned[:64]), halves(turned[64:])
        rows_ref[g * 64 : g * 64 + 64, :512] = jnp.concatenate([*first, *second], 1)
    copies[0].wait()
    for g in range(0, GROUP // 8, 4):
        found = dot(rows_ref[g * 64 : g * 64 + 256, :512], spread[...])
        for h in range(4):
            for k in range(8):
                at = (8 * (g + h) + k) * 64
                sticks_ref[at : at + 64, :] = found[h * 64 : h * 64 + 64, k * 128 : k * 128 + 128]
    copies[1].wait()

    def scatter(i, _):
        first = pl.multiple_of(i * 128, 128)
        for j in range(128):
            pltpu.store(
                square_ref.at[pl.ds(place_ref[i, j], 1), :],
                sticks_ref[pl.ds(first + j, 1), :],
                mask=(bits_ref[pl.ds(i * 16 + j // 8, 1), :] & (1 << (j % 8))) != 0,
            )
        return 0

    lax.fori_loop(0, STICKS // 128, scatter, 0)

    def turn(i, _):
        rows = pl.ds(pl.multiple_of(i * 128, 128), 128)
        turned_ref[rows, :] = square_ref[rows, :].T
        return 0

    lax.fori_loop(0, 32, turn, 0, unroll=4)
    pairs = [(b, p) for b in range(BANDS) for p in range(PLANES)]
    copies[2].wait()
    left = lane < HALF
    alone = (lane & (HALF - 1)) == 0
    for k, (b, p) in enumerate(pairs):
        sums = []
        ends = []
        for at in (b * 16 + p, b * 16 + 8 + 3 + p):
            x = turned_ref[pl.ds(at, 128, stride=32), :]
            mirror = pltpu.roll(x, HALF, 1)
            sums.append(jnp.where(alone, x, jnp.where(left, x, -x) + mirror))
            end = jnp.where(left, mirror, x)
            end_high = end.astype(BF16).astype(F32)
            ends.append(jnp.where(left, end - end_high, end_high).astype(BF16))
        real, imag = sums
        for i, x in enumerate((jnp.where(left, real, imag), jnp.where(left, imag, -real))):
            high, low = halves(x)
            rows_ref[k * 128 : k * 128 + 128, i * 512 : i * 512 + 512] = jnp.concatenate([high, low, high, ends[i]], 1)
        if k % 2 == 1:
            at = (k - 1) * 128
            for i in range(2):
                half_ref[at : at + 256, i * FINE : i * FINE + FINE] = dot(
                    rows_ref[at : at + 256, i * 512 : i * 512 + 512], row_up[...]
                )
    for copy in copies[3:]:
        copy.wait()
    for k, (b, p) in enumerate(pairs):
        upper = half_ref[k * 128 : k * 128 + HALF, :]
        lower = half_ref[k * 128 + HALF : k * 128 + 128, :]
        even = dot(even_up[...], folded_data(upper + bare_first(lower), lower))
        odd = dot(odd_up[...], folded_data(upper - lower, lower))
        odd_real, odd_imag = odd[:, :FINE], odd[:, FINE:]
        local = pot_ref[p]
        last = even[WIDTH : WIDTH + 8]
        even = even[:WIDTH]
        ahead = jnp.concatenate([even[:, :FINE] - odd_imag, even[:, FINE:] + odd_real], 1)
        behind = jnp.concatenate([even[:, :FINE] + odd_imag, even[:, FINE:] - odd_real], 1)
        behind = other_first(behind, last)
        ahead = ahead * jnp.concatenate([local[:WIDTH], local[:WIDTH]], 1)
        behind = behind * jnp.concatenate([local[WIDTH:], local[WIDTH:]], 1)
        even = dot(even_down[...], folded_data(ahead + bare_first(behind), behind))
        odd = dot(odd_down[...], folded_data(ahead - behind))
        odd_plus = bare_first(odd)
        last = even[HALF : HALF + 8]
        even = even[:HALF]
        even_minus = other_first(even, last)
        real = jnp.concatenate(
            [even[:, :FINE] + odd_plus[:, FINE:], even_minus[:, :FINE] - odd[:, FINE:]], 0
        )
        imag = jnp.concatenate(
            [even[:, FINE:] - odd_plus[:, :FINE], even_minus[:, FINE:] + odd[:, :FINE]], 0
        )
        rows_ref[k * 128 : k * 128 + 128, :] = data_rows(jnp.concatenate([real, imag], 1), 1)
        if k % 2 == 1:
            at = (k - 1) * 128
            back_ref[at : at + 256, :] = dot(rows_ref[at : at + 256, :], row_down[...])
    for k, (b, p) in enumerate(pairs):
        for c in range(2):
            turned_ref[pl.ds(b * 16 + c * 8 + p, 128, stride=32), :] = back_ref[
                k * 128 : k * 128 + 128, c * 128 : c * 128 + 128
            ]

    def turn_back(i, _):
        rows = pl.ds(pl.multiple_of(i * 128, 128), 128)
        square_ref[rows, :] = turned_ref[rows, :].T
        return 0

    lax.fori_loop(0, 32, turn_back, 0, unroll=4)

    def gather(i, _):
        first = pl.multiple_of(i * 128, 128)
        for j in range(128):
            sticks_ref[pl.ds(first + j, 1), :] = square_ref[pl.ds(place_ref[i, j], 1), :]
        return 0

    lax.fori_loop(0, STICKS // 128, gather, 0)
    own_bit = 1 << (lax.broadcasted_iota(jnp.int32, (256, 128), 0) & 7)
    for at in range(0, STICKS, 256):
        bits = jnp.broadcast_to(bits_ref[at // 8 : at // 8 + 32, :][:, None, :], (32, 8, 128)).reshape(256, 128)
        rows = jnp.where((bits & own_bit) != 0, sticks_ref[at : at + 256, :], 0.0)
        found = lax.dot_general(
            choose[...],
            jnp.concatenate(halves(rows), 1),
            (((1,), (1,)), ((), ())),
            preferred_element_type=F32,
        )
        for h in range(2):
            here = found[:, h * 128 : h * 128 + 128]
            swapped = pltpu.roll(here, 64, 1)
            for i, part in enumerate(
                (jnp.where(left, here[:16], swapped[16:]), jnp.where(left, swapped[:16], here[16:]))
            ):
                to = (at // 64 + 2 * h + i) * PARTS
                send_ref[to : to + PLANES, :] = part[:PLANES]
                send_ref[to + PLANES : to + PARTS, :] = part[8 : 8 + PLANES]


def after_kernel(map_ref, corr_ref, recv_ref, down_ref, out_ref):
    sticks = corr_ref.shape[1]
    kinetic = kinetic_of(map_ref, sticks)
    local = dot(down_ref[...], data_rows(recv_ref[...], 0))
    local = jnp.concatenate([local[:128].T, local[128:].T], 1)
    both = jnp.concatenate([kinetic, kinetic], 1)
    for b in range(BANDS):
        out_ref[b] = both * corr_ref[b] + local[b * sticks : (b + 1) * sticks]


def shape(*dims):
    return jax.ShapeDtypeStruct(dims, F32)


def exchange(values):
    values = values.reshape(GROUP, 1, PARTS * 128)
    return lax.all_to_all(values, "pw", 0, 0, tiled=True).reshape(GROUP * PARTS, 128)


def in_vmem(x):
    return pltpu.with_memory_space_constraint(x, pltpu.VMEM)


def in_hbm(x):
    return pltpu.with_memory_space_constraint(x, pltpu.HBM)


def cost(us):
    return pl.CostEstimate(flops=int(us * 1e9), bytes_accessed=int(us * 3e6), transcendentals=0)


def call(kernel, name, us, inputs, out_shape, in_specs, out_specs, scratch=()):
    return pl.pallas_call(
        kernel,
        out_shape=out_shape,
        in_specs=in_specs,
        out_specs=out_specs,
        scratch_shapes=list(scratch),
        compiler_params=PARAMS,
        cost_estimate=cost(us),
        name=name,
    )(*inputs)


def middle(place, received, local, mask, t):
    grid = BANDS * PLANES * 128
    names = ("spread", "row_up", "even_up", "odd_up", "even_down", "odd_down", "row_down", "choose")
    return call(
        middle_kernel,
        "middle",
        20,
        (in_hbm(place), in_vmem(received), in_vmem(local), in_vmem(mask), *(in_hbm(t[n]) for n in names)),
        pltpu.VMEM((GROUP * PARTS, 128), F32),
        [ANY, VMEM, VMEM, VMEM] + [ANY] * 8,
        VMEM,
        [
            pltpu.SMEM((STICKS // 128, 128), jnp.int32),
            pltpu.VMEM((STICKS, 128), F32),
            pltpu.VMEM((STICKS, 128), F32),
            pltpu.VMEM((STICKS, 128), F32),
            pltpu.VMEM((grid, 6 * FINE), BF16),
            pltpu.VMEM((grid, 2 * FINE), F32),
            pltpu.VMEM((grid, FINE), F32),
            *(pltpu.VMEM(t[n].shape, BF16) for n in names),
            pltpu.SemaphoreType.DMA((9,)),
        ],
    )


def prepare(rotation, map_rows, orbitals, correction, potential, t):
    bands, sticks, doubled = orbitals.shape
    return call(
        prepare_kernel,
        "prepare",
        7,
        tuple(
            in_hbm(x)
            for x in (rotation, map_rows, orbitals, correction, potential, t["fine_rows"], t["fine_cols"])
        ),
        (
            pltpu.VMEM((PLANES, FINE, FINE), F32),
            pltpu.VMEM((STICKS // 8, 128), jnp.int32),
            pltpu.HBM(map_rows.shape, jnp.int32),
            pltpu.VMEM((2, BANDS, sticks, doubled), F32),
            pltpu.VMEM((2, BANDS, sticks, doubled), F32),
        ),
        [SMEM, VMEM, VMEM, VMEM, ANY, VMEM, VMEM],
        (VMEM,) * 5,
        [
            pltpu.VMEM((PLANES * LENGTH, LENGTH), F32),
            pltpu.VMEM((PLANES, 3 * LENGTH, FINE), BF16),
            pltpu.SemaphoreType.DMA((PLANES,)),
        ],
    )


def on_device(orbitals, applied_orbitals, potential, stick_map, ritz_values, ritz_rotation):
    t = {name: jnp.asarray(value) for name, value in tables().items()}
    map_rows = stick_map.reshape(-1, 128)
    sent, correction = call(
        before_kernel,
        "before",
        2,
        tuple(in_hbm(x) for x in (ritz_values, map_rows, orbitals, applied_orbitals, t["stick_up"])),
        (pltpu.VMEM((GROUP * PARTS, 128), F32), pltpu.HBM(orbitals.shape, F32)),
        [SMEM] + [VMEM] * 4,
        (VMEM, VMEM),
    )
    received = exchange(sent)
    local, mask, place, kept, passed = prepare(ritz_rotation.T, map_rows, orbitals, correction, potential, t)
    came = lax.ppermute(passed, "bg", [(i, i ^ 1) for i in range(4)])
    product, came = lax.optimization_barrier((middle(place, received, local, mask, t), came))
    returned = exchange(product)
    halved = kept + came
    last = lax.ppermute(halved[1], "bg", [(i, 3 - i) for i in range(4)])
    applied_correction = call(
        after_kernel,
        "after",
        2,
        (in_vmem(map_rows), in_vmem(correction), in_vmem(returned), in_vmem(t["stick_down"])),
        shape(*orbitals.shape),
        [VMEM] * 4,
        VMEM,
    )
    applied_correction, last = lax.optimization_barrier((applied_correction, last))
    next_orbitals = halved[0] + last
    return (next_orbitals, applied_correction)


def solution(mesh):
    return jax.shard_map(
        on_device,
        mesh=mesh,
        in_specs=(P("bg", "pw", None), P("bg", "pw", None), P("pw", None, None), P(), P("bg"), P()),
        out_specs=(P("bg", "pw", None), P("bg", "pw", None)),
        check_vma=False,
    )
```

```python
import functools
import math

import jax
import jax.numpy as jnp
import ml_dtypes
import numpy as np
from jax import lax
from jax.experimental import pallas as pl
from jax.experimental.pallas import tpu as pltpu
from jax.sharding import PartitionSpec as P

F32 = jnp.float32
BF16 = jnp.bfloat16
VMEM = pl.BlockSpec(memory_space=pltpu.VMEM)
SMEM = pl.BlockSpec(memory_space=pltpu.SMEM)
ANY = pl.BlockSpec(memory_space=pl.ANY)
PARAMS = pltpu.CompilerParams(vmem_limit_bytes=32 * 1024 * 1024)

LENGTH = 320
WIDTH = 128
FINE = 2 * WIDTH
GROUP = 64
PLANES = LENGTH // GROUP
PARTS = 2 * PLANES
STICKS = GROUP * 64
BANDS = 2


def split_host(table):
    high = table.astype(ml_dtypes.bfloat16)
    low = (table - high.astype(np.float64)).astype(ml_dtypes.bfloat16)
    return high, low


HALF = WIDTH // 2


def frequency_slots():
    return np.concatenate([np.arange(HALF), [-HALF], -np.arange(1, HALF)])


def point_slots():
    return np.concatenate([np.arange(WIDTH), [WIDTH], -np.arange(1, WIDTH)])


def complex_table(frequencies, points, length):
    angles = 2.0 * math.pi * (np.outer(frequencies, points) % length) / length
    cosine, sine = np.cos(angles) / math.sqrt(length), np.sin(angles) / math.sqrt(length)
    return np.concatenate(
        [np.concatenate([cosine, sine], 1), np.concatenate([-sine, cosine], 1)], 0
    )


def wave(function, frequencies, points):
    angles = 2.0 * math.pi * (np.outer(frequencies, points) % FINE) / FINE
    return function(angles) / math.sqrt(FINE)


def folded_tables():
    zeros = np.zeros
    pairs, near = np.arange(HALF), np.arange(WIDTH)
    three = np.concatenate

    def joined(main, single):
        high, low = split_host(main)
        return three([high, high, low, single.astype(ml_dtypes.bfloat16)], 1)

    points = point_slots()
    sines = -wave(np.sin, pairs, points)
    sines[0] = wave(np.sin, [HALF], points)
    single = zeros((FINE, WIDTH))
    single[:, 0] = single[:, HALF] = wave(np.cos, [HALF], points)[0]
    row_up = joined(three([wave(np.cos, pairs, points), sines], 0).T, single).T
    single = zeros((WIDTH + 16, 16))
    single[: WIDTH + 1, 0] = single[: WIDTH + 1, 8] = wave(np.cos, [HALF], np.arange(WIDTH + 1))[0]
    even = zeros((WIDTH + 16, HALF))
    even[: WIDTH + 1] = wave(np.cos, pairs, np.arange(WIDTH + 1)).T
    even_up = joined(even, single)
    single = zeros((WIDTH, 16))
    single[:, 0] = single[:, 8] = -wave(np.sin, [HALF], near)[0]
    odd_up = joined(wave(np.sin, pairs, near).T, single)
    single = zeros((HALF + 16, 16))
    single[: HALF + 1, 0] = single[: HALF + 1, 8] = wave(np.cos, np.arange(HALF + 1), [WIDTH])[:, 0]
    even = zeros((HALF + 16, WIDTH))
    even[: HALF + 1] = wave(np.cos, np.arange(HALF + 1), near)
    even_down = joined(even, single)
    odd_high, odd_low = split_host(wave(np.sin, [HALF, *range(1, HALF)], near))
    odd_down = three([odd_high, odd_high, odd_low], 1)
    return dict(row_up=row_up, even_up=even_up, odd_up=odd_up, even_down=even_down, odd_down=odd_down)


def resampling_table():
    places = point_slots()[:, None] * LENGTH - np.arange(LENGTH)[None, :] * FINE
    total = np.zeros((FINE, LENGTH))
    for d in range(-(WIDTH - 1), WIDTH):
        total += np.cos(2.0 * math.pi * ((places * d) % (FINE * LENGTH)) / (FINE * LENGTH))
    return total / LENGTH


def spreading_table():
    table = np.zeros((2, 2, 8, 16, 8, 4, 2, 16))
    for b in range(2):
        for k in range(8):
            for part in range(16):
                table[b, :, k, part, k, :, b, part] = 1.0
    return table.reshape(512, 1024).astype(ml_dtypes.bfloat16)


def choosing_table():
    table = np.zeros((2, 16, 2, 4, 2, 16))
    for b in range(2):
        for part in range(16):
            table[b, part, :, :, b, part] = 1.0
    return table.reshape(32, 256).astype(ml_dtypes.bfloat16)


def tables():
    high, low = split_host(complex_table(frequency_slots(), point_slots(), FINE))
    stick = complex_table(np.arange(WIDTH) - HALF, np.arange(LENGTH), LENGTH).reshape(2 * WIDTH, 2, GROUP, PLANES)
    stick = stick.transpose(0, 2, 1, 3).reshape(2 * WIDTH, GROUP * PARTS)
    s_high, s_low = split_host(stick)
    r_high, r_low = split_host(resampling_table())
    three = np.concatenate
    return dict(
        **folded_tables(),
        row_down=three([high.T, high.T, low.T], 0),
        stick_up=three([s_high.T, s_low.T], 1),
        stick_down=three([s_high, s_low, s_high], 1),
        fine_cols=three([r_high, r_low, r_high, np.zeros((FINE, 64), r_high.dtype)], 1),
        spread=spreading_table(),
        choose=choosing_table(),
        fine_rows=three(
            [
                *(r.T[:FINE] for r in (r_high, r_high, r_low)),
                *(r.T[FINE:] for r in (r_high, r_high, r_low)),
                np.zeros((64, FINE), r_high.dtype),
            ],
            0,
        ),
    )


def halves(x):
    high = x.astype(BF16)
    low = (x - high.astype(F32)).astype(BF16)
    return high, low


def data_rows(x, axis):
    high, low = halves(x)
    return jnp.concatenate([high, high, low] if axis == 0 else [high, low, high], axis)


def dot(a, b):
    return jnp.dot(a, b, preferred_element_type=F32)


def slot_of(index):
    return jnp.where(index >= HALF, index - HALF, HALF + ((HALF - index) & (HALF - 1)))


def bare_first(x):
    first = lax.broadcasted_iota(jnp.int32, (8, 1), 0) == 0
    return jnp.concatenate([jnp.where(first, 0.0, x[:8]), x[8:]], 0)


def other_first(x, other):
    first = lax.broadcasted_iota(jnp.int32, (8, 1), 0) == 0
    return jnp.concatenate([jnp.where(first, other[:8], x[:8]), x[8:]], 0)


def folded_data(x, single=None):
    high, low = halves(x)
    parts = [high, low, high]
    if single is not None:
        top = single[:8]
        top_high = top.astype(BF16).astype(F32)
        parts.append(jnp.concatenate([top_high, top - top_high], 0).astype(BF16))
    return jnp.concatenate(parts, 0)


def planar_of(map_ref, sticks):
    me = lax.axis_index("pw")
    per_row = 128 // sticks
    row = map_ref[pl.ds(me // per_row, 1), :]
    fx = (row >> 7) - WIDTH // 2
    fy = (row & (WIDTH - 1)) - WIDTH // 2
    planar = (fx * fx + fy * fy).astype(F32)
    turned = jnp.broadcast_to(planar, (128, 128)).T
    upper = lax.rem(me, per_row) == 1
    return jnp.where(upper, turned[sticks:], turned[:sticks])


def kinetic_of(map_ref, sticks):
    planar = planar_of(map_ref, sticks)
    fz = lax.broadcasted_iota(jnp.int32, (1, WIDTH), 1) - WIDTH // 2
    return (planar + (fz * fz).astype(F32)) * (1.0 / (WIDTH // 2) ** 2)


def before_kernel(
    values_hbm, map_hbm, orb_hbm, app_hbm, up_hbm, send_ref, corr_hbm,
    values_ref, map_ref, orb_ref, app_ref, up_ref, corr_ref, sems,
):
    pairs = (
        (values_hbm, values_ref),
        (map_hbm, map_ref),
        (orb_hbm, orb_ref),
        (app_hbm, app_ref),
        (up_hbm, up_ref),
        (corr_ref, corr_hbm),
    )
    copies = [pltpu.make_async_copy(source, target, sems.at[i]) for i, (source, target) in enumerate(pairs)]
    for copy in copies[:5]:
        copy.start()
    for copy in copies[:4]:
        copy.wait()
    sticks = orb_ref.shape[1]
    kinetic = kinetic_of(map_ref, sticks)
    scale = 1.0 + jnp.concatenate([kinetic, kinetic], 1)
    corr = []
    for b in range(BANDS):
        c = (app_ref[b] - values_ref[b] * orb_ref[b]) / scale
        corr_ref[b] = c
        corr.append(c)
    copies[5].start()
    rows = jnp.concatenate(corr, 0)
    turned = jnp.concatenate([rows[:, :128].T, rows[:, 128:].T], 0)
    high, low = halves(turned)
    copies[4].wait()
    both = jnp.concatenate([high, high], 0)
    for at in range(0, GROUP * PARTS, 160):
        send_ref[at : at + 160, :] = dot(up_ref[at : at + 160, :], both) + dot(up_ref[at : at + 160, : 2 * WIDTH], low)
    copies[5].wait()


def prepare_kernel(
    rotation_hbm, map_hbm, orb_hbm, corr_hbm, pot_hbm, rows_hbm, cols_hbm, out_ref, bits_ref, place_ref, keep_ref, pass_ref,
    rotation_ref, map_ref, orb_ref, corr_ref, pot_ref, rows_ref, cols_ref, work_ref, sems,
):
    pairs = [
        (rotation_hbm, rotation_ref),
        (map_hbm, map_ref),
        (orb_hbm, orb_ref),
        (corr_hbm, corr_ref),
        (rows_hbm, rows_ref),
        *((pot_hbm.at[p], pot_ref.at[p]) for p in range(PLANES)),
        (cols_hbm, cols_ref),
    ]
    copies = [pltpu.make_async_copy(source, target, sems.at[i]) for i, (source, target) in enumerate(pairs)]
    for copy in copies:
        copy.start()
    for p in range(PLANES):
        work_ref[p, 3 * LENGTH :] = jnp.zeros((64, FINE), BF16)
    for copy in copies[:4]:
        copy.wait()
    me = lax.axis_index("bg")
    all_bands = rotation_ref.shape[0]
    for target, group in ((keep_ref, me), (pass_ref, me ^ 1)):
        for k, owner in enumerate((group, 3 - group)):
            for i in range(BANDS):
                j = owner * BANDS + i
                total = None
                for b in range(BANDS):
                    term = rotation_ref[j, me * BANDS + b] * orb_ref[b]
                    term = term + rotation_ref[j, all_bands + me * BANDS + b] * corr_ref[b]
                    total = term if total is None else total + term
                target[k, i] = total
    columns = slot_of(map_ref[...] >> 7)
    place_ref[...] = ((columns >> 2) << 7) | slot_of(map_ref[...] & 127)
    columns = columns & 3
    row_block = lax.broadcasted_iota(jnp.int32, (128, 128), 0) >> 5
    stick = lax.broadcasted_iota(jnp.int32, (16, 128), 1)
    eight = lax.broadcasted_iota(jnp.int32, (16, 128), 0)
    weights = jnp.where((stick >> 3) == eight, (1 << (stick & 7)).astype(F32), 0.0).astype(BF16)
    marked = 0
    copies[4].wait()
    for p in range(PLANES):
        copies[5 + p].wait()
        for at in range(0, LENGTH, LENGTH // 2):
            end = at + LENGTH // 2
            high, low = halves(pot_ref[p, at:end, :FINE])
            rest = pot_ref[p, at:end, FINE:]
            rest_high = rest.astype(BF16).astype(F32)
            rest = jnp.concatenate([rest_high, rest - rest_high, rest_high, jnp.zeros_like(rest)], 1)
            part = dot(jnp.concatenate([high, low, high, rest.astype(BF16)], 1), rows_ref[...])
            high, low = halves(part)
            for k, values in enumerate((high, high, low)):
                work_ref[p, k * LENGTH + at : k * LENGTH + end] = values
            for _ in range(4):
                if marked < STICKS // 128:
                    match = jnp.where(columns[marked : marked + 1, :] == row_block, 1.0, 0.0).astype(BF16)
                    bits = lax.dot_general(weights, match, (((1,), (1,)), ((), ())), preferred_element_type=F32)
                    bits_ref[marked * 16 : marked * 16 + 16, :] = bits.astype(jnp.int32)
                    marked += 1
        if p == 0:
            copies[5 + PLANES].wait()
        out_ref[p] = dot(cols_ref[...], work_ref[p])


def middle_kernel(
    place_hbm, recv_ref, pot_ref, bits_ref, spread_hbm, row_up_hbm, even_up_hbm, odd_up_hbm, even_down_hbm,
    odd_down_hbm, row_down_hbm, choose_hbm,
    send_hbm,
    send_ref, place_ref, sticks_ref, square_ref, turned_ref, rows_ref, half_ref, back_ref,
    spread, row_up, even_up, odd_up, even_down, odd_down, row_down, choose, sems,
):
    copies = [
        pltpu.make_async_copy(source, target, sems.at[i])
        for i, (source, target) in enumerate(
            (
                (spread_hbm, spread),
                (place_hbm, place_ref),
                (row_up_hbm, row_up),
                (even_up_hbm, even_up),
                (odd_up_hbm, odd_up),
                (even_down_hbm, even_down),
                (odd_down_hbm, odd_down),
                (row_down_hbm, row_down),
                (choose_hbm, choose),
            )
        )
    ]
    for copy in copies:
        copy.start()
    square_ref[...] = jnp.zeros_like(square_ref)
    lane = lax.broadcasted_iota(jnp.int32, (1, 128), 1)

    for g in range(GROUP // 8):
        parts = []
        for d in range(8 * g, 8 * g + 8):
            parts += [recv_ref[d * PARTS : d * PARTS + 8, :], recv_ref[d * PARTS + 2 : d * PARTS + 10, :]]
        turned = jnp.concatenate(parts, 0).T
        first, second = halves(turned[:64]), halves(turned[64:])
        rows_ref[g * 64 : g * 64 + 64, :512] = jnp.concatenate([*first, *second], 1)
    copies[0].wait()
    for g in range(0, GROUP // 8, 4):
        found = dot(rows_ref[g * 64 : g * 64 + 256, :512], spread[...])
        for h in range(4):
            for k in range(8):
                at = (8 * (g + h) + k) * 64
                sticks_ref[at : at + 64, :] = found[h * 64 : h * 64 + 64, k * 128 : k * 128 + 128]
    copies[1].wait()

    def scatter(i, _):
        first = pl.multiple_of(i * 128, 128)
        for j in range(128):
            pltpu.store(
                square_ref.at[pl.ds(place_ref[i, j], 1), :],
                sticks_ref[pl.ds(first + j, 1), :],
                mask=(bits_ref[pl.ds(i * 16 + j // 8, 1), :] & (1 << (j % 8))) != 0,
            )
        return 0

    lax.fori_loop(0, STICKS // 128, scatter, 0)

    def turn(i, _):
        rows = pl.ds(pl.multiple_of(i * 128, 128), 128)
        turned_ref[rows, :] = square_ref[rows, :].T
        return 0

    lax.fori_loop(0, 32, turn, 0, unroll=4)
    pairs = [(b, p) for b in range(BANDS) for p in range(PLANES)]
    copies[2].wait()
    left = lane < HALF
    alone = (lane & (HALF - 1)) == 0
    for k, (b, p) in enumerate(pairs):
        sums = []
        ends = []
        for at in (b * 16 + p, b * 16 + 8 + 3 + p):
            x = turned_ref[pl.ds(at, 128, stride=32), :]
            mirror = pltpu.roll(x, HALF, 1)
            sums.append(jnp.where(alone, x, jnp.where(left, x, -x) + mirror))
            end = jnp.where(left, mirror, x)
            end_high = end.astype(BF16).astype(F32)
            ends.append(jnp.where(left, end - end_high, end_high).astype(BF16))
        real, imag = sums
        for i, x in enumerate((jnp.where(left, real, imag), jnp.where(left, imag, -real))):
            high, low = halves(x)
            rows_ref[k * 128 : k * 128 + 128, i * 512 : i * 512 + 512] = jnp.concatenate([high, low, high, ends[i]], 1)
        if k % 2 == 1:
            at = (k - 1) * 128
            for i in range(2):
                half_ref[at : at + 256, i * FINE : i * FINE + FINE] = dot(
                    rows_ref[at : at + 256, i * 512 : i * 512 + 512], row_up[...]
                )
    for copy in copies[3:]:
        copy.wait()
    for k, (b, p) in enumerate(pairs):
        upper = half_ref[k * 128 : k * 128 + HALF, :]
        lower = half_ref[k * 128 + HALF : k * 128 + 128, :]
        even = dot(even_up[...], folded_data(upper + bare_first(lower), lower))
        odd = dot(odd_up[...], folded_data(upper - lower, lower))
        odd_real, odd_imag = odd[:, :FINE], odd[:, FINE:]
        local = pot_ref[p]
        last = even[WIDTH : WIDTH + 8]
        even = even[:WIDTH]
        ahead = jnp.concatenate([even[:, :FINE] - odd_imag, even[:, FINE:] + odd_real], 1)
        behind = jnp.concatenate([even[:, :FINE] + odd_imag, even[:, FINE:] - odd_real], 1)
        behind = other_first(behind, last)
        ahead = ahead * jnp.concatenate([local[:WIDTH], local[:WIDTH]], 1)
        behind = behind * jnp.concatenate([local[WIDTH:], local[WIDTH:]], 1)
        even = dot(even_down[...], folded_data(ahead + bare_first(behind), behind))
        odd = dot(odd_down[...], folded_data(ahead - behind))
        odd_plus = bare_first(odd)
        last = even[HALF : HALF + 8]
        even = even[:HALF]
        even_minus = other_first(even, last)
        real = jnp.concatenate(
            [even[:, :FINE] + odd_plus[:, FINE:], even_minus[:, :FINE] - odd[:, FINE:]], 0
        )
        imag = jnp.concatenate(
            [even[:, FINE:] - odd_plus[:, :FINE], even_minus[:, FINE:] + odd[:, :FINE]], 0
        )
        rows_ref[k * 128 : k * 128 + 128, :] = data_rows(jnp.concatenate([real, imag], 1), 1)
        if k % 2 == 1:
            at = (k - 1) * 128
            back_ref[at : at + 256, :] = dot(rows_ref[at : at + 256, :], row_down[...])
    for k, (b, p) in enumerate(pairs):
        for c in range(2):
            turned_ref[pl.ds(b * 16 + c * 8 + p, 128, stride=32), :] = back_ref[
                k * 128 : k * 128 + 128, c * 128 : c * 128 + 128
            ]

    def turn_back(i, _):
        rows = pl.ds(pl.multiple_of(i * 128, 128), 128)
        square_ref[rows, :] = turned_ref[rows, :].T
        return 0

    lax.fori_loop(0, 32, turn_back, 0, unroll=4)

    def gather(i, _):
        first = pl.multiple_of(i * 128, 128)
        for j in range(128):
            sticks_ref[pl.ds(first + j, 1), :] = square_ref[pl.ds(place_ref[i, j], 1), :]
        return 0

    lax.fori_loop(0, STICKS // 128, gather, 0)
    sent = []
    own_bit = 1 << (lax.broadcasted_iota(jnp.int32, (256, 128), 0) & 7)
    for at in range(0, STICKS, 256):
        bits = jnp.broadcast_to(bits_ref[at // 8 : at // 8 + 32, :][:, None, :], (32, 8, 128)).reshape(256, 128)
        rows = jnp.where((bits & own_bit) != 0, sticks_ref[at : at + 256, :], 0.0)
        found = lax.dot_general(
            choose[...],
            jnp.concatenate(halves(rows), 1),
            (((1,), (1,)), ((), ())),
            preferred_element_type=F32,
        )
        for h in range(2):
            here = found[:, h * 128 : h * 128 + 128]
            swapped = pltpu.roll(here, 64, 1)
            for i, part in enumerate(
                (jnp.where(left, here[:16], swapped[16:]), jnp.where(left, swapped[:16], here[16:]))
            ):
                to = (at // 64 + 2 * h + i) * PARTS
                send_ref[to : to + PLANES, :] = part[:PLANES]
                send_ref[to + PLANES : to + PARTS, :] = part[8 : 8 + PLANES]
        if at % 1024 == 768:
            part = pl.ds((at - 768) // 64 * PARTS, 16 * PARTS)
            sent.append(pltpu.make_async_copy(send_ref.at[part, :], send_hbm.at[part, :], sems.at[9 + len(sent)]))
            sent[-1].start()
    for copy in sent:
        copy.wait()


def after_kernel(map_ref, corr_ref, recv_ref, down_ref, out_ref):
    sticks = corr_ref.shape[1]
    kinetic = kinetic_of(map_ref, sticks)
    local = dot(down_ref[...], data_rows(recv_ref[...], 0))
    local = jnp.concatenate([local[:128].T, local[128:].T], 1)
    both = jnp.concatenate([kinetic, kinetic], 1)
    for b in range(BANDS):
        out_ref[b] = both * corr_ref[b] + local[b * sticks : (b + 1) * sticks]


def shape(*dims):
    return jax.ShapeDtypeStruct(dims, F32)


def exchange(values):
    values = values.reshape(GROUP, 1, PARTS * 128)
    return lax.all_to_all(values, "pw", 0, 0, tiled=True).reshape(GROUP * PARTS, 128)


def in_vmem(x):
    return pltpu.with_memory_space_constraint(x, pltpu.VMEM)


def in_hbm(x):
    return pltpu.with_memory_space_constraint(x, pltpu.HBM)


def cost(us):
    return pl.CostEstimate(flops=int(us * 1e9), bytes_accessed=int(us * 3e6), transcendentals=0)


def call(kernel, name, us, inputs, out_shape, in_specs, out_specs, scratch=()):
    return pl.pallas_call(
        kernel,
        out_shape=out_shape,
        in_specs=in_specs,
        out_specs=out_specs,
        scratch_shapes=list(scratch),
        compiler_params=PARAMS,
        cost_estimate=cost(us),
        name=name,
    )(*inputs)


def middle(place, received, local, mask, t):
    grid = BANDS * PLANES * 128
    names = ("spread", "row_up", "even_up", "odd_up", "even_down", "odd_down", "row_down", "choose")
    return call(
        middle_kernel,
        "middle",
        20,
        (in_hbm(place), in_vmem(received), in_vmem(local), in_vmem(mask), *(in_hbm(t[n]) for n in names)),
        pltpu.HBM((GROUP * PARTS, 128), F32),
        [ANY, VMEM, VMEM, VMEM] + [ANY] * 8,
        ANY,
        [
            pltpu.VMEM((GROUP * PARTS, 128), F32),
            pltpu.SMEM((STICKS // 128, 128), jnp.int32),
            pltpu.VMEM((STICKS, 128), F32),
            pltpu.VMEM((STICKS, 128), F32),
            pltpu.VMEM((STICKS, 128), F32),
            pltpu.VMEM((grid, 6 * FINE), BF16),
            pltpu.VMEM((grid, 2 * FINE), F32),
            pltpu.VMEM((grid, FINE), F32),
            *(pltpu.VMEM(t[n].shape, BF16) for n in names),
            pltpu.SemaphoreType.DMA((13,)),
        ],
    )


def prepare(rotation, map_rows, orbitals, correction, potential, t):
    bands, sticks, doubled = orbitals.shape
    return call(
        prepare_kernel,
        "prepare",
        7,
        tuple(
            in_hbm(x)
            for x in (rotation, map_rows, orbitals, correction, potential, t["fine_rows"], t["fine_cols"])
        ),
        (
            pltpu.VMEM((PLANES, FINE, FINE), F32),
            pltpu.VMEM((STICKS // 8, 128), jnp.int32),
            pltpu.HBM(map_rows.shape, jnp.int32),
            pltpu.VMEM((2, BANDS, sticks, doubled), F32),
            pltpu.VMEM((2, BANDS, sticks, doubled), F32),
        ),
        [ANY] * 7,
        (VMEM,) * 5,
        [
            pltpu.SMEM(rotation.shape, F32),
            pltpu.VMEM(map_rows.shape, jnp.int32),
            pltpu.VMEM(orbitals.shape, F32),
            pltpu.VMEM(orbitals.shape, F32),
            pltpu.VMEM((PLANES, LENGTH, LENGTH), F32),
            pltpu.VMEM(t["fine_rows"].shape, BF16),
            pltpu.VMEM(t["fine_cols"].shape, BF16),
            pltpu.VMEM((PLANES, 3 * LENGTH + 64, FINE), BF16),
            pltpu.SemaphoreType.DMA((PLANES + 6,)),
        ],
    )


def on_device(orbitals, applied_orbitals, potential, stick_map, ritz_values, ritz_rotation):
    t = {name: jnp.asarray(value) for name, value in tables().items()}
    map_rows = stick_map.reshape(-1, 128)
    sent, correction = call(
        before_kernel,
        "before",
        2,
        tuple(in_hbm(x) for x in (ritz_values, map_rows, orbitals, applied_orbitals, t["stick_up"])),
        (pltpu.VMEM((GROUP * PARTS, 128), F32), pltpu.HBM(orbitals.shape, F32)),
        [ANY] * 5,
        (VMEM, ANY),
        [
            pltpu.SMEM(ritz_values.shape, F32),
            pltpu.VMEM(map_rows.shape, jnp.int32),
            pltpu.VMEM(orbitals.shape, F32),
            pltpu.VMEM(orbitals.shape, F32),
            pltpu.VMEM(t["stick_up"].shape, BF16),
            pltpu.VMEM(orbitals.shape, F32),
            pltpu.SemaphoreType.DMA((6,)),
        ],
    )
    received = exchange(sent)
    local, mask, place, kept, passed = prepare(ritz_rotation.T, map_rows, orbitals, correction, potential, t)
    came = lax.ppermute(passed, "bg", [(i, i ^ 1) for i in range(4)])
    product, came = lax.optimization_barrier((middle(place, received, local, mask, t), came))
    returned = exchange(product)
    halved = kept + came
    last = lax.ppermute(halved[1], "bg", [(i, 3 - i) for i in range(4)])
    applied_correction = call(
        after_kernel,
        "after",
        2,
        (in_vmem(map_rows), in_vmem(correction), in_vmem(returned), in_vmem(t["stick_down"])),
        shape(*orbitals.shape),
        [VMEM] * 4,
        VMEM,
    )
    applied_correction, last = lax.optimization_barrier((applied_correction, last))
    next_orbitals = halved[0] + last
    return (next_orbitals, applied_correction)


def solution(mesh):
    return jax.shard_map(
        on_device,
        mesh=mesh,
        in_specs=(P("bg", "pw", None), P("bg", "pw", None), P("pw", None, None), P(), P("bg"), P()),
        out_specs=(P("bg", "pw", None), P("bg", "pw", None)),
        check_vma=False,
    )
```

```python
import functools
import math

import jax
import jax.numpy as jnp
import ml_dtypes
import numpy as np
from jax import lax
from jax.experimental import pallas as pl
from jax.experimental.pallas import tpu as pltpu
from jax.sharding import PartitionSpec as P

F32 = jnp.float32
BF16 = jnp.bfloat16
VMEM = pl.BlockSpec(memory_space=pltpu.VMEM)
SMEM = pl.BlockSpec(memory_space=pltpu.SMEM)
ANY = pl.BlockSpec(memory_space=pl.ANY)
PARAMS = pltpu.CompilerParams(vmem_limit_bytes=32 * 1024 * 1024)

LENGTH = 320
WIDTH = 128
FINE = 2 * WIDTH
GROUP = 64
PLANES = LENGTH // GROUP
PARTS = 2 * PLANES
STICKS = GROUP * 64
BANDS = 2


def split_host(table):
    high = table.astype(ml_dtypes.bfloat16)
    low = (table - high.astype(np.float64)).astype(ml_dtypes.bfloat16)
    return high, low


HALF = WIDTH // 2


def frequency_slots():
    return np.concatenate([np.arange(HALF), [-HALF], -np.arange(1, HALF)])


def point_slots():
    return np.concatenate([np.arange(WIDTH), [WIDTH], -np.arange(1, WIDTH)])


def complex_table(frequencies, points, length):
    angles = 2.0 * math.pi * (np.outer(frequencies, points) % length) / length
    cosine, sine = np.cos(angles) / math.sqrt(length), np.sin(angles) / math.sqrt(length)
    return np.concatenate(
        [np.concatenate([cosine, sine], 1), np.concatenate([-sine, cosine], 1)], 0
    )


def wave(function, frequencies, points):
    angles = 2.0 * math.pi * (np.outer(frequencies, points) % FINE) / FINE
    return function(angles) / math.sqrt(FINE)


def folded_tables():
    zeros = np.zeros
    pairs, near = np.arange(HALF), np.arange(WIDTH)
    three = np.concatenate

    def joined(main, single):
        high, low = split_host(main)
        return three([high, high, low, single.astype(ml_dtypes.bfloat16)], 1)

    points = point_slots()
    sines = -wave(np.sin, pairs, points)
    sines[0] = wave(np.sin, [HALF], points)
    single = zeros((FINE, WIDTH))
    single[:, 0] = single[:, HALF] = wave(np.cos, [HALF], points)[0]
    row_up = joined(three([wave(np.cos, pairs, points), sines], 0).T, single).T
    single = zeros((WIDTH + 16, 16))
    single[: WIDTH + 1, 0] = single[: WIDTH + 1, 8] = wave(np.cos, [HALF], np.arange(WIDTH + 1))[0]
    even = zeros((WIDTH + 16, HALF))
    even[: WIDTH + 1] = wave(np.cos, pairs, np.arange(WIDTH + 1)).T
    even_up = joined(even, single)
    single = zeros((WIDTH, 16))
    single[:, 0] = single[:, 8] = -wave(np.sin, [HALF], near)[0]
    odd_up = joined(wave(np.sin, pairs, near).T, single)
    single = zeros((HALF + 16, 16))
    single[: HALF + 1, 0] = single[: HALF + 1, 8] = wave(np.cos, np.arange(HALF + 1), [WIDTH])[:, 0]
    even = zeros((HALF + 16, WIDTH))
    even[: HALF + 1] = wave(np.cos, np.arange(HALF + 1), near)
    even_down = joined(even, single)
    odd_high, odd_low = split_host(wave(np.sin, [HALF, *range(1, HALF)], near))
    odd_down = three([odd_high, odd_high, odd_low], 1)
    return dict(row_up=row_up, even_up=even_up, odd_up=odd_up, even_down=even_down, odd_down=odd_down)


def resampling_table():
    places = point_slots()[:, None] * LENGTH - np.arange(LENGTH)[None, :] * FINE
    total = np.zeros((FINE, LENGTH))
    for d in range(-(WIDTH - 1), WIDTH):
        total += np.cos(2.0 * math.pi * ((places * d) % (FINE * LENGTH)) / (FINE * LENGTH))
    return total / LENGTH


def spreading_table():
    table = np.zeros((2, 2, 8, 16, 8, 4, 2, 16))
    for b in range(2):
        for k in range(8):
            for part in range(16):
                table[b, :, k, part, k, :, b, part] = 1.0
    return table.reshape(512, 1024).astype(ml_dtypes.bfloat16)


def tables():
    high, low = split_host(complex_table(frequency_slots(), point_slots(), FINE))
    stick = complex_table(np.arange(WIDTH) - HALF, np.arange(LENGTH), LENGTH).reshape(2 * WIDTH, 2, GROUP, PLANES)
    stick = stick.transpose(0, 2, 1, 3).reshape(2 * WIDTH, GROUP * PARTS)
    s_high, s_low = split_host(stick)
    r_high, r_low = split_host(resampling_table())
    three = np.concatenate
    return dict(
        **folded_tables(),
        row_down=three([high.T, high.T, low.T], 0),
        stick_up=three([s_high.T, s_low.T], 1),
        stick_down=three([s_high, s_low, s_high], 1),
        fine_cols=three([r_high, r_low, r_high, np.zeros((FINE, 64), r_high.dtype)], 1),
        spread=spreading_table(),
        same=np.tile(np.eye(128), (1, 2)).astype(ml_dtypes.bfloat16),
        fine_rows=three(
            [
                *(r.T[:FINE] for r in (r_high, r_high, r_low)),
                *(r.T[FINE:] for r in (r_high, r_high, r_low)),
                np.zeros((64, FINE), r_high.dtype),
            ],
            0,
        ),
    )


def halves(x):
    high = x.astype(BF16)
    low = (x - high.astype(F32)).astype(BF16)
    return high, low


def data_rows(x, axis):
    high, low = halves(x)
    return jnp.concatenate([high, high, low] if axis == 0 else [high, low, high], axis)


def dot(a, b):
    return jnp.dot(a, b, preferred_element_type=F32)


def slot_of(index):
    return jnp.where(index >= HALF, index - HALF, HALF + ((HALF - index) & (HALF - 1)))


def bare_first(x):
    first = lax.broadcasted_iota(jnp.int32, (8, 1), 0) == 0
    return jnp.concatenate([jnp.where(first, 0.0, x[:8]), x[8:]], 0)


def other_first(x, other):
    first = lax.broadcasted_iota(jnp.int32, (8, 1), 0) == 0
    return jnp.concatenate([jnp.where(first, other[:8], x[:8]), x[8:]], 0)


def folded_data(x, single=None):
    high, low = halves(x)
    parts = [high, low, high]
    if single is not None:
        top = single[:8]
        top_high = top.astype(BF16).astype(F32)
        parts.append(jnp.concatenate([top_high, top - top_high], 0).astype(BF16))
    return jnp.concatenate(parts, 0)


def planar_of(map_ref, sticks):
    me = lax.axis_index("pw")
    per_row = 128 // sticks
    row = map_ref[pl.ds(me // per_row, 1), :]
    fx = (row >> 7) - WIDTH // 2
    fy = (row & (WIDTH - 1)) - WIDTH // 2
    planar = (fx * fx + fy * fy).astype(F32)
    turned = jnp.broadcast_to(planar, (128, 128)).T
    upper = lax.rem(me, per_row) == 1
    return jnp.where(upper, turned[sticks:], turned[:sticks])


def kinetic_of(map_ref, sticks):
    planar = planar_of(map_ref, sticks)
    fz = lax.broadcasted_iota(jnp.int32, (1, WIDTH), 1) - WIDTH // 2
    return (planar + (fz * fz).astype(F32)) * (1.0 / (WIDTH // 2) ** 2)


def before_kernel(
    values_hbm, map_hbm, orb_hbm, app_hbm, up_hbm, send_ref, corr_hbm,
    values_ref, map_ref, orb_ref, app_ref, up_ref, corr_ref, sems,
):
    pairs = (
        (values_hbm, values_ref),
        (map_hbm, map_ref),
        (orb_hbm, orb_ref),
        (app_hbm, app_ref),
        (up_hbm, up_ref),
        (corr_ref, corr_hbm),
    )
    copies = [pltpu.make_async_copy(source, target, sems.at[i]) for i, (source, target) in enumerate(pairs)]
    for copy in copies[:5]:
        copy.start()
    for copy in copies[:4]:
        copy.wait()
    sticks = orb_ref.shape[1]
    kinetic = kinetic_of(map_ref, sticks)
    scale = 1.0 + jnp.concatenate([kinetic, kinetic], 1)
    corr = []
    for b in range(BANDS):
        c = (app_ref[b] - values_ref[b] * orb_ref[b]) / scale
        corr_ref[b] = c
        corr.append(c)
    copies[5].start()
    rows = jnp.concatenate(corr, 0)
    turned = jnp.concatenate([rows[:, :128].T, rows[:, 128:].T], 0)
    high, low = halves(turned)
    copies[4].wait()
    both = jnp.concatenate([high, high], 0)
    for at in range(0, GROUP * PARTS, 160):
        send_ref[at : at + 160, :] = dot(up_ref[at : at + 160, :], both) + dot(up_ref[at : at + 160, : 2 * WIDTH], low)
    copies[5].wait()


def prepare_kernel(
    rotation_hbm, map_hbm, orb_hbm, corr_hbm, pot_hbm, rows_hbm, cols_hbm, out_ref, bits_ref, block_ref, place_ref, keep_ref, pass_ref,
    rotation_ref, map_ref, orb_ref, corr_ref, pot_ref, rows_ref, cols_ref, work_ref, sems,
):
    pairs = [
        (rotation_hbm, rotation_ref),
        (map_hbm, map_ref),
        (orb_hbm, orb_ref),
        (corr_hbm, corr_ref),
        (rows_hbm, rows_ref),
        *((pot_hbm.at[p], pot_ref.at[p]) for p in range(PLANES)),
        (cols_hbm, cols_ref),
    ]
    copies = [pltpu.make_async_copy(source, target, sems.at[i]) for i, (source, target) in enumerate(pairs)]
    for copy in copies:
        copy.start()
    for p in range(PLANES):
        work_ref[p, 3 * LENGTH :] = jnp.zeros((64, FINE), BF16)
    for copy in copies[:4]:
        copy.wait()
    me = lax.axis_index("bg")
    all_bands = rotation_ref.shape[0]
    for target, group in ((keep_ref, me), (pass_ref, me ^ 1)):
        for k, owner in enumerate((group, 3 - group)):
            for i in range(BANDS):
                j = owner * BANDS + i
                total = None
                for b in range(BANDS):
                    term = rotation_ref[j, me * BANDS + b] * orb_ref[b]
                    term = term + rotation_ref[j, all_bands + me * BANDS + b] * corr_ref[b]
                    total = term if total is None else total + term
                target[k, i] = total
    columns = slot_of(map_ref[...] >> 7)
    place_ref[...] = ((columns >> 2) << 7) | slot_of(map_ref[...] & 127)
    columns = columns & 3
    block_ref[...] = columns
    row_block = lax.broadcasted_iota(jnp.int32, (128, 128), 0) >> 5
    stick = lax.broadcasted_iota(jnp.int32, (16, 128), 1)
    eight = lax.broadcasted_iota(jnp.int32, (16, 128), 0)
    weights = jnp.where((stick >> 3) == eight, (1 << (stick & 7)).astype(F32), 0.0).astype(BF16)
    marked = 0
    copies[4].wait()
    for p in range(PLANES):
        copies[5 + p].wait()
        for at in range(0, LENGTH, LENGTH // 2):
            end = at + LENGTH // 2
            high, low = halves(pot_ref[p, at:end, :FINE])
            rest = pot_ref[p, at:end, FINE:]
            rest_high = rest.astype(BF16).astype(F32)
            rest = jnp.concatenate([rest_high, rest - rest_high, rest_high, jnp.zeros_like(rest)], 1)
            part = dot(jnp.concatenate([high, low, high, rest.astype(BF16)], 1), rows_ref[...])
            high, low = halves(part)
            for k, values in enumerate((high, high, low)):
                work_ref[p, k * LENGTH + at : k * LENGTH + end] = values
            for _ in range(4):
                if marked < STICKS // 128:
                    match = jnp.where(columns[marked : marked + 1, :] == row_block, 1.0, 0.0).astype(BF16)
                    bits = lax.dot_general(weights, match, (((1,), (1,)), ((), ())), preferred_element_type=F32)
                    bits_ref[marked * 16 : marked * 16 + 16, :] = bits.astype(jnp.int32)
                    marked += 1
        if p == 0:
            copies[5 + PLANES].wait()
        out_ref[p] = dot(cols_ref[...], work_ref[p])


def across(same, x):
    both = jnp.concatenate(halves(x), 1)
    return lax.dot_general(same[...], both, (((1,), (1,)), ((), ())), preferred_element_type=F32)


def middle_kernel(
    place_hbm, recv_ref, pot_ref, bits_ref, block_hbm, spread_hbm, row_up_hbm, even_up_hbm, odd_up_hbm, even_down_hbm,
    odd_down_hbm, row_down_hbm, same_hbm,
    send_hbm,
    send_ref, place_ref, block_ref, sticks_ref, square_ref, turned_ref, rows_ref, half_ref, back_ref,
    spread, row_up, even_up, odd_up, even_down, odd_down, row_down, same, sems,
):
    copies = [
        pltpu.make_async_copy(source, target, sems.at[i])
        for i, (source, target) in enumerate(
            (
                (spread_hbm, spread),
                (place_hbm, place_ref),
                (row_up_hbm, row_up),
                (even_up_hbm, even_up),
                (odd_up_hbm, odd_up),
                (even_down_hbm, even_down),
                (odd_down_hbm, odd_down),
                (row_down_hbm, row_down),
                (same_hbm, same),
                (block_hbm, block_ref),
            )
        )
    ]
    for copy in copies:
        copy.start()
    square_ref[...] = jnp.zeros_like(square_ref)
    lane = lax.broadcasted_iota(jnp.int32, (1, 128), 1)

    for g in range(GROUP // 8):
        parts = []
        for d in range(8 * g, 8 * g + 8):
            parts += [recv_ref[d * PARTS : d * PARTS + 8, :], recv_ref[d * PARTS + 2 : d * PARTS + 10, :]]
        turned = jnp.concatenate(parts, 0).T
        first, second = halves(turned[:64]), halves(turned[64:])
        rows_ref[g * 64 : g * 64 + 64, :512] = jnp.concatenate([*first, *second], 1)
    copies[0].wait()
    for g in range(0, GROUP // 8, 4):
        found = dot(rows_ref[g * 64 : g * 64 + 256, :512], spread[...])
        for h in range(4):
            for k in range(8):
                at = (8 * (g + h) + k) * 64
                sticks_ref[at : at + 64, :] = found[h * 64 : h * 64 + 64, k * 128 : k * 128 + 128]
    copies[1].wait()

    def scatter(i, _):
        first = pl.multiple_of(i * 128, 128)
        for j in range(128):
            pltpu.store(
                square_ref.at[pl.ds(place_ref[i, j], 1), :],
                sticks_ref[pl.ds(first + j, 1), :],
                mask=(bits_ref[pl.ds(i * 16 + j // 8, 1), :] & (1 << (j % 8))) != 0,
            )
        return 0

    lax.fori_loop(0, STICKS // 128, scatter, 0)

    for at in range(0, STICKS, 128):
        turned_ref[at : at + 128, :] = square_ref[at : at + 128, :].T
    pairs = [(b, p) for b in range(BANDS) for p in range(PLANES)]
    copies[2].wait()
    left = lane < HALF
    alone = (lane & (HALF - 1)) == 0
    for k, (b, p) in enumerate(pairs):
        sums = []
        ends = []
        for at in (b * 16 + p, b * 16 + 8 + 3 + p):
            x = turned_ref[pl.ds(at, 128, stride=32), :]
            mirror = pltpu.roll(x, HALF, 1)
            sums.append(jnp.where(alone, x, jnp.where(left, x, -x) + mirror))
            end = jnp.where(left, mirror, x)
            end_high = end.astype(BF16).astype(F32)
            ends.append(jnp.where(left, end - end_high, end_high).astype(BF16))
        real, imag = sums
        for i, x in enumerate((jnp.where(left, real, imag), jnp.where(left, imag, -real))):
            high, low = halves(x)
            rows_ref[k * 128 : k * 128 + 128, i * 512 : i * 512 + 512] = jnp.concatenate([high, low, high, ends[i]], 1)
        if k % 2 == 1:
            at = (k - 1) * 128
            for i in range(2):
                half_ref[at : at + 256, i * FINE : i * FINE + FINE] = dot(
                    rows_ref[at : at + 256, i * 512 : i * 512 + 512], row_up[...]
                )
    for copy in copies[3:]:
        copy.wait()
    for k, (b, p) in enumerate(pairs):
        upper = half_ref[k * 128 : k * 128 + HALF, :]
        lower = half_ref[k * 128 + HALF : k * 128 + 128, :]
        even = dot(even_up[...], folded_data(upper + bare_first(lower), lower))
        odd = dot(odd_up[...], folded_data(upper - lower, lower))
        odd_real, odd_imag = odd[:, :FINE], odd[:, FINE:]
        local = pot_ref[p]
        last = even[WIDTH : WIDTH + 8]
        even = even[:WIDTH]
        ahead = jnp.concatenate([even[:, :FINE] - odd_imag, even[:, FINE:] + odd_real], 1)
        behind = jnp.concatenate([even[:, :FINE] + odd_imag, even[:, FINE:] - odd_real], 1)
        behind = other_first(behind, last)
        ahead = ahead * jnp.concatenate([local[:WIDTH], local[:WIDTH]], 1)
        behind = behind * jnp.concatenate([local[WIDTH:], local[WIDTH:]], 1)
        even = dot(even_down[...], folded_data(ahead + bare_first(behind), behind))
        odd = dot(odd_down[...], folded_data(ahead - behind))
        odd_plus = bare_first(odd)
        last = even[HALF : HALF + 8]
        even = even[:HALF]
        even_minus = other_first(even, last)
        real = jnp.concatenate(
            [even[:, :FINE] + odd_plus[:, FINE:], even_minus[:, :FINE] - odd[:, FINE:]], 0
        )
        imag = jnp.concatenate(
            [even[:, FINE:] - odd_plus[:, :FINE], even_minus[:, FINE:] + odd[:, :FINE]], 0
        )
        rows_ref[k * 128 : k * 128 + 128, :] = data_rows(jnp.concatenate([real, imag], 1), 1)
        if k % 2 == 1:
            at = (k - 1) * 128
            back_ref[at : at + 256, :] = dot(rows_ref[at : at + 256, :], row_down[...])
    for k, (b, p) in enumerate(pairs):
        for c in range(2):
            turned_ref[pl.ds(b * 16 + c * 8 + p, 128, stride=32), :] = back_ref[
                k * 128 : k * 128 + 128, c * 128 : c * 128 + 128
            ]

    for at in range(0, STICKS, 128):
        square_ref[at : at + 128, :] = turned_ref[at : at + 128, :].T

    def gather(i, _):
        first = pl.multiple_of(i * 128, 128)
        for j in range(128):
            sticks_ref[pl.ds(first + j, 1), :] = square_ref[pl.ds(place_ref[i, j], 1), :]
        return 0

    lax.fori_loop(0, STICKS // 128, gather, 0)
    sent = []
    left = lane < 64
    for at in range(0, STICKS, 256):
        every = across(same, sticks_ref[at : at + 256, :])
        own = jnp.concatenate([block_ref[at // 128 + i : at // 128 + i + 1, :] for i in range(2)], 1)
        found = every[:32]
        for h in range(1, 4):
            found = jnp.where(own == h, every[32 * h : 32 * h + 32], found)
        for h in range(2):
            here = found[:, h * 128 : h * 128 + 128]
            swapped = pltpu.roll(here, 64, 1)
            for i, part in enumerate(
                (jnp.where(left, here[:16], swapped[16:]), jnp.where(left, swapped[:16], here[16:]))
            ):
                to = (at // 64 + 2 * h + i) * PARTS
                send_ref[to : to + PLANES, :] = part[:PLANES]
                send_ref[to + PLANES : to + PARTS, :] = part[8 : 8 + PLANES]
        if at % 1024 == 768:
            part = pl.ds((at - 768) // 64 * PARTS, 16 * PARTS)
            sent.append(pltpu.make_async_copy(send_ref.at[part, :], send_hbm.at[part, :], sems.at[10 + len(sent)]))
            sent[-1].start()
    for copy in sent:
        copy.wait()


def after_kernel(map_ref, corr_ref, recv_ref, down_ref, out_ref):
    sticks = corr_ref.shape[1]
    kinetic = kinetic_of(map_ref, sticks)
    local = dot(down_ref[...], data_rows(recv_ref[...], 0))
    local = jnp.concatenate([local[:128].T, local[128:].T], 1)
    both = jnp.concatenate([kinetic, kinetic], 1)
    for b in range(BANDS):
        out_ref[b] = both * corr_ref[b] + local[b * sticks : (b + 1) * sticks]


def shape(*dims):
    return jax.ShapeDtypeStruct(dims, F32)


def exchange(values):
    values = values.reshape(GROUP, 1, PARTS * 128)
    return lax.all_to_all(values, "pw", 0, 0, tiled=True).reshape(GROUP * PARTS, 128)


def in_vmem(x):
    return pltpu.with_memory_space_constraint(x, pltpu.VMEM)


def in_hbm(x):
    return pltpu.with_memory_space_constraint(x, pltpu.HBM)


def cost(us):
    return pl.CostEstimate(flops=int(us * 1e9), bytes_accessed=int(us * 3e6), transcendentals=0)


def call(kernel, name, us, inputs, out_shape, in_specs, out_specs, scratch=()):
    return pl.pallas_call(
        kernel,
        out_shape=out_shape,
        in_specs=in_specs,
        out_specs=out_specs,
        scratch_shapes=list(scratch),
        compiler_params=PARAMS,
        cost_estimate=cost(us),
        name=name,
    )(*inputs)


def middle(place, received, local, bits, block, t):
    grid = BANDS * PLANES * 128
    names = ("spread", "row_up", "even_up", "odd_up", "even_down", "odd_down", "row_down", "same")
    return call(
        middle_kernel,
        "middle",
        20,
        (in_hbm(place), in_vmem(received), in_vmem(local), in_vmem(bits), in_hbm(block), *(in_hbm(t[n]) for n in names)),
        pltpu.HBM((GROUP * PARTS, 128), F32),
        [ANY] + [VMEM] * 3 + [ANY] * 9,
        ANY,
        [
            pltpu.VMEM((GROUP * PARTS, 128), F32),
            pltpu.SMEM((STICKS // 128, 128), jnp.int32),
            pltpu.VMEM((STICKS // 128, 128), jnp.int32),
            pltpu.VMEM((STICKS, 128), F32),
            pltpu.VMEM((STICKS, 128), F32),
            pltpu.VMEM((STICKS, 128), F32),
            pltpu.VMEM((grid, 6 * FINE), BF16),
            pltpu.VMEM((grid, 2 * FINE), F32),
            pltpu.VMEM((grid, FINE), F32),
            *(pltpu.VMEM(t[n].shape, BF16) for n in names),
            pltpu.SemaphoreType.DMA((14,)),
        ],
    )


def prepare(rotation, map_rows, orbitals, correction, potential, t):
    bands, sticks, doubled = orbitals.shape
    return call(
        prepare_kernel,
        "prepare",
        7,
        tuple(
            in_hbm(x)
            for x in (rotation, map_rows, orbitals, correction, potential, t["fine_rows"], t["fine_cols"])
        ),
        (
            pltpu.VMEM((PLANES, FINE, FINE), F32),
            pltpu.VMEM((STICKS // 8, 128), jnp.int32),
            pltpu.HBM(map_rows.shape, jnp.int32),
            pltpu.HBM(map_rows.shape, jnp.int32),
            pltpu.VMEM((2, BANDS, sticks, doubled), F32),
            pltpu.VMEM((2, BANDS, sticks, doubled), F32),
        ),
        [ANY] * 7,
        (VMEM,) * 6,
        [
            pltpu.SMEM(rotation.shape, F32),
            pltpu.VMEM(map_rows.shape, jnp.int32),
            pltpu.VMEM(orbitals.shape, F32),
            pltpu.VMEM(orbitals.shape, F32),
            pltpu.VMEM((PLANES, LENGTH, LENGTH), F32),
            pltpu.VMEM(t["fine_rows"].shape, BF16),
            pltpu.VMEM(t["fine_cols"].shape, BF16),
            pltpu.VMEM((PLANES, 3 * LENGTH + 64, FINE), BF16),
            pltpu.SemaphoreType.DMA((PLANES + 6,)),
        ],
    )


def on_device(orbitals, applied_orbitals, potential, stick_map, ritz_values, ritz_rotation):
    t = {name: jnp.asarray(value) for name, value in tables().items()}
    map_rows = stick_map.reshape(-1, 128)
    sent, correction = call(
        before_kernel,
        "before",
        2,
        tuple(in_hbm(x) for x in (ritz_values, map_rows, orbitals, applied_orbitals, t["stick_up"])),
        (pltpu.VMEM((GROUP * PARTS, 128), F32), pltpu.HBM(orbitals.shape, F32)),
        [ANY] * 5,
        (VMEM, ANY),
        [
            pltpu.SMEM(ritz_values.shape, F32),
            pltpu.VMEM(map_rows.shape, jnp.int32),
            pltpu.VMEM(orbitals.shape, F32),
            pltpu.VMEM(orbitals.shape, F32),
            pltpu.VMEM(t["stick_up"].shape, BF16),
            pltpu.VMEM(orbitals.shape, F32),
            pltpu.SemaphoreType.DMA((6,)),
        ],
    )
    received = exchange(sent)
    local, bits, block, place, kept, passed = prepare(ritz_rotation.T, map_rows, orbitals, correction, potential, t)
    came = lax.ppermute(passed, "bg", [(i, i ^ 1) for i in range(4)])
    product, came = lax.optimization_barrier((middle(place, received, local, bits, block, t), came))
    returned = exchange(product)
    halved = kept + came
    last = lax.ppermute(halved[1], "bg", [(i, 3 - i) for i in range(4)])
    applied_correction = call(
        after_kernel,
        "after",
        2,
        (in_vmem(map_rows), in_vmem(correction), in_vmem(returned), in_vmem(t["stick_down"])),
        shape(*orbitals.shape),
        [VMEM] * 4,
        VMEM,
    )
    applied_correction, last = lax.optimization_barrier((applied_correction, last))
    next_orbitals = halved[0] + last
    return (next_orbitals, applied_correction)


def solution(mesh):
    return jax.shard_map(
        on_device,
        mesh=mesh,
        in_specs=(P("bg", "pw", None), P("bg", "pw", None), P("pw", None, None), P(), P("bg"), P()),
        out_specs=(P("bg", "pw", None), P("bg", "pw", None)),
        check_vma=False,
    )
```

```python
import functools
import math

import jax
import jax.numpy as jnp
import ml_dtypes
import numpy as np
from jax import lax
from jax.experimental import pallas as pl
from jax.experimental.pallas import tpu as pltpu
from jax.sharding import PartitionSpec as P

F32 = jnp.float32
BF16 = jnp.bfloat16
VMEM = pl.BlockSpec(memory_space=pltpu.VMEM)
SMEM = pl.BlockSpec(memory_space=pltpu.SMEM)
ANY = pl.BlockSpec(memory_space=pl.ANY)
PARAMS = pltpu.CompilerParams(vmem_limit_bytes=32 * 1024 * 1024)

LENGTH = 320
WIDTH = 128
FINE = 2 * WIDTH
GROUP = 64
PLANES = LENGTH // GROUP
PARTS = 2 * PLANES
STICKS = GROUP * 64
BANDS = 2


def split_host(table):
    high = table.astype(ml_dtypes.bfloat16)
    low = (table - high.astype(np.float64)).astype(ml_dtypes.bfloat16)
    return high, low


HALF = WIDTH // 2


def frequency_slots():
    return np.concatenate([np.arange(HALF), [-HALF], -np.arange(1, HALF)])


def point_slots():
    return np.concatenate([np.arange(WIDTH), [WIDTH], -np.arange(1, WIDTH)])


def complex_table(frequencies, points, length):
    angles = 2.0 * math.pi * (np.outer(frequencies, points) % length) / length
    cosine, sine = np.cos(angles) / math.sqrt(length), np.sin(angles) / math.sqrt(length)
    return np.concatenate(
        [np.concatenate([cosine, sine], 1), np.concatenate([-sine, cosine], 1)], 0
    )


def wave(function, frequencies, points):
    angles = 2.0 * math.pi * (np.outer(frequencies, points) % FINE) / FINE
    return function(angles) / math.sqrt(FINE)


def folded_tables():
    zeros = np.zeros
    pairs, near = np.arange(HALF), np.arange(WIDTH)
    three = np.concatenate

    def joined(main, single):
        high, low = split_host(main)
        return three([high, high, low, single.astype(ml_dtypes.bfloat16)], 1)

    points = point_slots()
    sines = -wave(np.sin, pairs, points)
    sines[0] = wave(np.sin, [HALF], points)
    single = zeros((FINE, WIDTH))
    single[:, 0] = single[:, HALF] = wave(np.cos, [HALF], points)[0]
    row_up = joined(three([wave(np.cos, pairs, points), sines], 0).T, single).T
    single = zeros((WIDTH + 16, 16))
    single[: WIDTH + 1, 0] = single[: WIDTH + 1, 8] = wave(np.cos, [HALF], np.arange(WIDTH + 1))[0]
    even = zeros((WIDTH + 16, HALF))
    even[: WIDTH + 1] = wave(np.cos, pairs, np.arange(WIDTH + 1)).T
    even_up = joined(even, single)
    single = zeros((WIDTH, 16))
    single[:, 0] = single[:, 8] = -wave(np.sin, [HALF], near)[0]
    odd_up = joined(wave(np.sin, pairs, near).T, single)
    single = zeros((HALF + 16, 16))
    single[: HALF + 1, 0] = single[: HALF + 1, 8] = wave(np.cos, np.arange(HALF + 1), [WIDTH])[:, 0]
    even = zeros((HALF + 16, WIDTH))
    even[: HALF + 1] = wave(np.cos, np.arange(HALF + 1), near)
    even_down = joined(even, single)
    odd_high, odd_low = split_host(wave(np.sin, [HALF, *range(1, HALF)], near))
    odd_down = three([odd_high, odd_high, odd_low], 1)
    return dict(row_up=row_up, even_up=even_up, odd_up=odd_up, even_down=even_down, odd_down=odd_down)


def resampling_table():
    places = point_slots()[:, None] * LENGTH - np.arange(LENGTH)[None, :] * FINE
    total = np.zeros((FINE, LENGTH))
    for d in range(-(WIDTH - 1), WIDTH):
        total += np.cos(2.0 * math.pi * ((places * d) % (FINE * LENGTH)) / (FINE * LENGTH))
    return total / LENGTH


def spreading_table():
    table = np.zeros((2, 2, 8, 16, 8, 4, 2, 16))
    for b in range(2):
        for k in range(8):
            for part in range(16):
                table[b, :, k, part, k, :, b, part] = 1.0
    return table.reshape(512, 1024).astype(ml_dtypes.bfloat16)


def tables():
    high, low = split_host(complex_table(frequency_slots(), point_slots(), FINE))
    stick = complex_table(np.arange(WIDTH) - HALF, np.arange(LENGTH), LENGTH).reshape(2 * WIDTH, 2, GROUP, PLANES)
    stick = stick.transpose(0, 2, 1, 3).reshape(2 * WIDTH, GROUP * PARTS)
    s_high, s_low = split_host(stick)
    r_high, r_low = split_host(resampling_table())
    three = np.concatenate
    return dict(
        **folded_tables(),
        row_down=three([high.T, high.T, low.T], 0),
        stick_up=three([s_high.T, s_low.T], 1),
        stick_down=three([s_high, s_low, s_high], 1),
        fine_cols=three([r_high, r_low, r_high, np.zeros((FINE, 64), r_high.dtype)], 1),
        spread=spreading_table(),
        same=np.tile(np.eye(128), (1, 2)).astype(ml_dtypes.bfloat16),
        fine_rows=three(
            [
                *(r.T[:FINE] for r in (r_high, r_high, r_low)),
                *(r.T[FINE:] for r in (r_high, r_high, r_low)),
                np.zeros((64, FINE), r_high.dtype),
            ],
            0,
        ),
    )


def halves(x):
    high = x.astype(BF16)
    low = (x - high.astype(F32)).astype(BF16)
    return high, low


def data_rows(x, axis):
    high, low = halves(x)
    return jnp.concatenate([high, high, low] if axis == 0 else [high, low, high], axis)


def dot(a, b):
    return jnp.dot(a, b, preferred_element_type=F32)


def slot_of(index):
    return jnp.where(index >= HALF, index - HALF, HALF + ((HALF - index) & (HALF - 1)))


def bare_first(x):
    first = lax.broadcasted_iota(jnp.int32, (8, 1), 0) == 0
    return jnp.concatenate([jnp.where(first, 0.0, x[:8]), x[8:]], 0)


def other_first(x, other):
    first = lax.broadcasted_iota(jnp.int32, (8, 1), 0) == 0
    return jnp.concatenate([jnp.where(first, other[:8], x[:8]), x[8:]], 0)


def folded_data(x, single=None):
    high, low = halves(x)
    parts = [high, low, high]
    if single is not None:
        top = single[:8]
        top_high = top.astype(BF16).astype(F32)
        parts.append(jnp.concatenate([top_high, top - top_high], 0).astype(BF16))
    return jnp.concatenate(parts, 0)


def planar_of(map_ref, sticks):
    me = lax.axis_index("pw")
    per_row = 128 // sticks
    row = map_ref[pl.ds(me // per_row, 1), :]
    fx = (row >> 7) - WIDTH // 2
    fy = (row & (WIDTH - 1)) - WIDTH // 2
    planar = (fx * fx + fy * fy).astype(F32)
    turned = jnp.broadcast_to(planar, (128, 128)).T
    upper = lax.rem(me, per_row) == 1
    return jnp.where(upper, turned[sticks:], turned[:sticks])


def kinetic_of(map_ref, sticks):
    planar = planar_of(map_ref, sticks)
    fz = lax.broadcasted_iota(jnp.int32, (1, WIDTH), 1) - WIDTH // 2
    return (planar + (fz * fz).astype(F32)) * (1.0 / (WIDTH // 2) ** 2)


def before_kernel(
    values_hbm, map_hbm, orb_hbm, app_hbm, up_hbm, send_ref, corr_hbm,
    values_ref, map_ref, orb_ref, app_ref, up_ref, corr_ref, sems,
):
    pairs = (
        (values_hbm, values_ref),
        (map_hbm, map_ref),
        (orb_hbm, orb_ref),
        (app_hbm, app_ref),
        (up_hbm, up_ref),
        (corr_ref, corr_hbm),
    )
    copies = [pltpu.make_async_copy(source, target, sems.at[i]) for i, (source, target) in enumerate(pairs)]
    for copy in copies[:5]:
        copy.start()
    for copy in copies[:4]:
        copy.wait()
    sticks = orb_ref.shape[1]
    kinetic = kinetic_of(map_ref, sticks)
    scale = 1.0 + jnp.concatenate([kinetic, kinetic], 1)
    corr = []
    for b in range(BANDS):
        c = (app_ref[b] - values_ref[b] * orb_ref[b]) / scale
        corr_ref[b] = c
        corr.append(c)
    copies[5].start()
    rows = jnp.concatenate(corr, 0)
    turned = jnp.concatenate([rows[:, :128].T, rows[:, 128:].T], 0)
    high, low = halves(turned)
    copies[4].wait()
    both = jnp.concatenate([high, high], 0)
    for at in range(0, GROUP * PARTS, 160):
        send_ref[at : at + 160, :] = dot(up_ref[at : at + 160, :], both) + dot(up_ref[at : at + 160, : 2 * WIDTH], low)
    copies[5].wait()


def prepare_kernel(
    rotation_hbm, map_hbm, orb_hbm, corr_hbm, pot_hbm, rows_hbm, cols_hbm, out_ref, bits_ref, block_ref, place_ref, keep_ref, pass_ref,
    rotation_ref, map_ref, orb_ref, corr_ref, pot_ref, rows_ref, cols_ref, work_ref, sems,
):
    pairs = [
        (rotation_hbm, rotation_ref),
        (map_hbm, map_ref),
        (orb_hbm, orb_ref),
        (corr_hbm, corr_ref),
        (rows_hbm, rows_ref),
        *((pot_hbm.at[p], pot_ref.at[p]) for p in range(PLANES)),
        (cols_hbm, cols_ref),
    ]
    copies = [pltpu.make_async_copy(source, target, sems.at[i]) for i, (source, target) in enumerate(pairs)]
    for copy in copies:
        copy.start()
    for p in range(PLANES):
        work_ref[p, 3 * LENGTH :] = jnp.zeros((64, FINE), BF16)
    for copy in copies[:4]:
        copy.wait()
    me = lax.axis_index("bg")
    all_bands = rotation_ref.shape[0]
    for target, group in ((keep_ref, me), (pass_ref, me ^ 1)):
        for k, owner in enumerate((group, 3 - group)):
            for i in range(BANDS):
                j = owner * BANDS + i
                total = None
                for b in range(BANDS):
                    term = rotation_ref[j, me * BANDS + b] * orb_ref[b]
                    term = term + rotation_ref[j, all_bands + me * BANDS + b] * corr_ref[b]
                    total = term if total is None else total + term
                target[k, i] = total
    columns = slot_of(map_ref[...] >> 7)
    place_ref[...] = ((columns >> 2) << 7) | slot_of(map_ref[...] & 127)
    columns = columns & 3
    block_ref[...] = columns
    row_block = lax.broadcasted_iota(jnp.int32, (128, 128), 0) >> 5
    stick = lax.broadcasted_iota(jnp.int32, (16, 128), 1)
    eight = lax.broadcasted_iota(jnp.int32, (16, 128), 0)
    weights = jnp.where((stick >> 3) == eight, (1 << (stick & 7)).astype(F32), 0.0).astype(BF16)
    marked = 0
    copies[4].wait()
    for p in range(PLANES):
        copies[5 + p].wait()
        for at in range(0, LENGTH, LENGTH // 2):
            end = at + LENGTH // 2
            high, low = halves(pot_ref[p, at:end, :FINE])
            rest = pot_ref[p, at:end, FINE:]
            rest_high = rest.astype(BF16).astype(F32)
            rest = jnp.concatenate([rest_high, rest - rest_high, rest_high, jnp.zeros_like(rest)], 1)
            part = dot(jnp.concatenate([high, low, high, rest.astype(BF16)], 1), rows_ref[...])
            high, low = halves(part)
            for k, values in enumerate((high, high, low)):
                work_ref[p, k * LENGTH + at : k * LENGTH + end] = values
            for _ in range(4):
                if marked < STICKS // 128:
                    match = jnp.where(columns[marked : marked + 1, :] == row_block, 1.0, 0.0).astype(BF16)
                    bits = lax.dot_general(weights, match, (((1,), (1,)), ((), ())), preferred_element_type=F32)
                    bits_ref[marked * 16 : marked * 16 + 16, :] = bits.astype(jnp.int32)
                    marked += 1
        if p == 0:
            copies[5 + PLANES].wait()
        out_ref[p] = dot(cols_ref[...], work_ref[p])


def across(same, x):
    both = jnp.concatenate(halves(x), 1)
    return lax.dot_general(same[...], both, (((1,), (1,)), ((), ())), preferred_element_type=F32)


def middle_kernel(
    place_hbm, recv_ref, pot_ref, bits_ref, block_hbm, spread_hbm, row_up_hbm, even_up_hbm, odd_up_hbm, even_down_hbm,
    odd_down_hbm, row_down_hbm, same_hbm,
    send_hbm,
    send_ref, place_ref, block_ref, sticks_ref, square_ref, turned_ref, rows_ref, half_ref, back_ref,
    spread, row_up, even_up, odd_up, even_down, odd_down, row_down, same, sems,
):
    copies = [
        pltpu.make_async_copy(source, target, sems.at[i])
        for i, (source, target) in enumerate(
            (
                (spread_hbm, spread),
                (place_hbm, place_ref),
                (row_up_hbm, row_up),
                (even_up_hbm, even_up),
                (odd_up_hbm, odd_up),
                (even_down_hbm, even_down),
                (odd_down_hbm, odd_down),
                (row_down_hbm, row_down),
                (same_hbm, same),
                (block_hbm, block_ref),
            )
        )
    ]
    for copy in copies:
        copy.start()
    square_ref[...] = jnp.zeros_like(square_ref)
    lane = lax.broadcasted_iota(jnp.int32, (1, 128), 1)

    for g in range(GROUP // 8):
        parts = []
        for d in range(8 * g, 8 * g + 8):
            parts += [recv_ref[d * PARTS : d * PARTS + 8, :], recv_ref[d * PARTS + 2 : d * PARTS + 10, :]]
        turned = jnp.concatenate(parts, 0).T
        first, second = halves(turned[:64]), halves(turned[64:])
        rows_ref[g * 64 : g * 64 + 64, :512] = jnp.concatenate([*first, *second], 1)
    copies[0].wait()
    for g in range(0, GROUP // 8, 4):
        found = dot(rows_ref[g * 64 : g * 64 + 256, :512], spread[...])
        for h in range(4):
            for k in range(8):
                at = (8 * (g + h) + k) * 64
                sticks_ref[at : at + 64, :] = found[h * 64 : h * 64 + 64, k * 128 : k * 128 + 128]
    copies[1].wait()

    def scatter(i, _):
        first = pl.multiple_of(i * 128, 128)
        for j in range(128):
            pltpu.store(
                square_ref.at[pl.ds(place_ref[i, j], 1), :],
                sticks_ref[pl.ds(first + j, 1), :],
                mask=(bits_ref[pl.ds(i * 16 + j // 8, 1), :] & (1 << (j % 8))) != 0,
            )
        return 0

    lax.fori_loop(0, STICKS // 128, scatter, 0)

    for at in range(0, STICKS, 128):
        turned_ref[at : at + 128, :] = square_ref[at : at + 128, :].T
    pairs = [(b, p) for b in range(BANDS) for p in range(PLANES)]
    copies[2].wait()
    left = lane < HALF
    alone = (lane & (HALF - 1)) == 0
    for k, (b, p) in enumerate(pairs):
        sums = []
        ends = []
        for at in (b * 16 + p, b * 16 + 8 + 3 + p):
            x = turned_ref[pl.ds(at, 128, stride=32), :]
            mirror = pltpu.roll(x, HALF, 1)
            sums.append(jnp.where(alone, x, jnp.where(left, x, -x) + mirror))
            end = jnp.where(left, mirror, x)
            end_high = end.astype(BF16).astype(F32)
            ends.append(jnp.where(left, end - end_high, end_high).astype(BF16))
        real, imag = sums
        for i, x in enumerate((jnp.where(left, real, imag), jnp.where(left, imag, -real))):
            high, low = halves(x)
            rows_ref[k * 128 : k * 128 + 128, i * 512 : i * 512 + 512] = jnp.concatenate([high, low, high, ends[i]], 1)
        if k % 2 == 1:
            at = (k - 1) * 128
            for i in range(2):
                half_ref[at : at + 256, i * FINE : i * FINE + FINE] = dot(
                    rows_ref[at : at + 256, i * 512 : i * 512 + 512], row_up[...]
                )
    for copy in copies[3:]:
        copy.wait()
    for k, (b, p) in enumerate(pairs):
        upper = half_ref[k * 128 : k * 128 + HALF, :]
        lower = half_ref[k * 128 + HALF : k * 128 + 128, :]
        even = dot(even_up[...], folded_data(upper + bare_first(lower), lower))
        odd = dot(odd_up[...], folded_data(upper - lower, lower))
        odd_real, odd_imag = odd[:, :FINE], odd[:, FINE:]
        local = pot_ref[p]
        last = even[WIDTH : WIDTH + 8]
        even = even[:WIDTH]
        ahead = jnp.concatenate([even[:, :FINE] - odd_imag, even[:, FINE:] + odd_real], 1)
        behind = jnp.concatenate([even[:, :FINE] + odd_imag, even[:, FINE:] - odd_real], 1)
        behind = other_first(behind, last)
        ahead = ahead * jnp.concatenate([local[:WIDTH], local[:WIDTH]], 1)
        behind = behind * jnp.concatenate([local[WIDTH:], local[WIDTH:]], 1)
        even = dot(even_down[...], folded_data(ahead + bare_first(behind), behind))
        odd = dot(odd_down[...], folded_data(ahead - behind))
        odd_plus = bare_first(odd)
        last = even[HALF : HALF + 8]
        even = even[:HALF]
        even_minus = other_first(even, last)
        real = jnp.concatenate(
            [even[:, :FINE] + odd_plus[:, FINE:], even_minus[:, :FINE] - odd[:, FINE:]], 0
        )
        imag = jnp.concatenate(
            [even[:, FINE:] - odd_plus[:, :FINE], even_minus[:, FINE:] + odd[:, :FINE]], 0
        )
        rows_ref[k * 128 : k * 128 + 128, :] = data_rows(jnp.concatenate([real, imag], 1), 1)
        if k % 2 == 1:
            at = (k - 1) * 128
            back_ref[at : at + 256, :] = dot(rows_ref[at : at + 256, :], row_down[...])
    for k, (b, p) in enumerate(pairs):
        for c in range(2):
            turned_ref[pl.ds(b * 16 + c * 8 + p, 128, stride=32), :] = back_ref[
                k * 128 : k * 128 + 128, c * 128 : c * 128 + 128
            ]

    for at in range(0, STICKS, 128):
        square_ref[at : at + 128, :] = turned_ref[at : at + 128, :].T

    def gather(i, _):
        first = pl.multiple_of(i * 128, 128)
        for j in range(128):
            sticks_ref[pl.ds(first + j, 1), :] = square_ref[pl.ds(place_ref[i, j], 1), :]
        return 0

    lax.fori_loop(0, STICKS // 128, gather, 0)
    sent = []
    left = lane < 64
    for at in range(0, STICKS, 256):
        every = across(same, sticks_ref[at : at + 256, :])
        own = jnp.concatenate([block_ref[at // 128 + i : at // 128 + i + 1, :] for i in range(2)], 1)
        found = every[:32]
        for h in range(1, 4):
            found = jnp.where(own == h, every[32 * h : 32 * h + 32], found)
        for h in range(2):
            here = found[:, h * 128 : h * 128 + 128]
            swapped = pltpu.roll(here, 64, 1)
            for i, part in enumerate(
                (jnp.where(left, here[:16], swapped[16:]), jnp.where(left, swapped[:16], here[16:]))
            ):
                to = (at // 64 + 2 * h + i) * PARTS
                send_ref[to : to + PLANES, :] = part[:PLANES]
                send_ref[to + PLANES : to + PARTS, :] = part[8 : 8 + PLANES]
        if at % 1024 == 768:
            part = pl.ds((at - 768) // 64 * PARTS, 16 * PARTS)
            sent.append(pltpu.make_async_copy(send_ref.at[part, :], send_hbm.at[part, :], sems.at[10 + len(sent)]))
            sent[-1].start()
    for copy in sent:
        copy.wait()


def after_kernel(map_ref, corr_ref, recv_ref, down_ref, mine_ref, last_ref, out_ref, next_ref):
    sticks = corr_ref.shape[1]
    kinetic = kinetic_of(map_ref, sticks)
    local = dot(down_ref[...], data_rows(recv_ref[...], 0))
    local = jnp.concatenate([local[:128].T, local[128:].T], 1)
    both = jnp.concatenate([kinetic, kinetic], 1)
    for b in range(BANDS):
        out_ref[b] = both * corr_ref[b] + local[b * sticks : (b + 1) * sticks]
        next_ref[b] = mine_ref[b] + last_ref[b]


def shape(*dims):
    return jax.ShapeDtypeStruct(dims, F32)


def exchange(values):
    values = values.reshape(GROUP, 1, PARTS * 128)
    return lax.all_to_all(values, "pw", 0, 0, tiled=True).reshape(GROUP * PARTS, 128)


def in_vmem(x):
    return pltpu.with_memory_space_constraint(x, pltpu.VMEM)


def in_hbm(x):
    return pltpu.with_memory_space_constraint(x, pltpu.HBM)


def cost(us):
    return pl.CostEstimate(flops=int(us * 1e9), bytes_accessed=int(us * 3e6), transcendentals=0)


def call(kernel, name, us, inputs, out_shape, in_specs, out_specs, scratch=()):
    return pl.pallas_call(
        kernel,
        out_shape=out_shape,
        in_specs=in_specs,
        out_specs=out_specs,
        scratch_shapes=list(scratch),
        compiler_params=PARAMS,
        cost_estimate=cost(us),
        name=name,
    )(*inputs)


def middle(place, received, local, bits, block, t):
    grid = BANDS * PLANES * 128
    names = ("spread", "row_up", "even_up", "odd_up", "even_down", "odd_down", "row_down", "same")
    return call(
        middle_kernel,
        "middle",
        20,
        (in_hbm(place), in_vmem(received), in_vmem(local), in_vmem(bits), in_hbm(block), *(in_hbm(t[n]) for n in names)),
        pltpu.HBM((GROUP * PARTS, 128), F32),
        [ANY] + [VMEM] * 3 + [ANY] * 9,
        ANY,
        [
            pltpu.VMEM((GROUP * PARTS, 128), F32),
            pltpu.SMEM((STICKS // 128, 128), jnp.int32),
            pltpu.VMEM((STICKS // 128, 128), jnp.int32),
            pltpu.VMEM((STICKS, 128), F32),
            pltpu.VMEM((STICKS, 128), F32),
            pltpu.VMEM((STICKS, 128), F32),
            pltpu.VMEM((grid, 6 * FINE), BF16),
            pltpu.VMEM((grid, 2 * FINE), F32),
            pltpu.VMEM((grid, FINE), F32),
            *(pltpu.VMEM(t[n].shape, BF16) for n in names),
            pltpu.SemaphoreType.DMA((14,)),
        ],
    )


def prepare(rotation, map_rows, orbitals, correction, potential, t):
    bands, sticks, doubled = orbitals.shape
    return call(
        prepare_kernel,
        "prepare",
        7,
        tuple(
            in_hbm(x)
            for x in (rotation, map_rows, orbitals, correction, potential, t["fine_rows"], t["fine_cols"])
        ),
        (
            pltpu.VMEM((PLANES, FINE, FINE), F32),
            pltpu.VMEM((STICKS // 8, 128), jnp.int32),
            pltpu.HBM(map_rows.shape, jnp.int32),
            pltpu.HBM(map_rows.shape, jnp.int32),
            pltpu.VMEM((2, BANDS, sticks, doubled), F32),
            pltpu.VMEM((2, BANDS, sticks, doubled), F32),
        ),
        [ANY] * 7,
        (VMEM,) * 6,
        [
            pltpu.SMEM(rotation.shape, F32),
            pltpu.VMEM(map_rows.shape, jnp.int32),
            pltpu.VMEM(orbitals.shape, F32),
            pltpu.VMEM(orbitals.shape, F32),
            pltpu.VMEM((PLANES, LENGTH, LENGTH), F32),
            pltpu.VMEM(t["fine_rows"].shape, BF16),
            pltpu.VMEM(t["fine_cols"].shape, BF16),
            pltpu.VMEM((PLANES, 3 * LENGTH + 64, FINE), BF16),
            pltpu.SemaphoreType.DMA((PLANES + 6,)),
        ],
    )


def on_device(orbitals, applied_orbitals, potential, stick_map, ritz_values, ritz_rotation):
    t = {name: jnp.asarray(value) for name, value in tables().items()}
    map_rows = stick_map.reshape(-1, 128)
    sent, correction = call(
        before_kernel,
        "before",
        2,
        tuple(in_hbm(x) for x in (ritz_values, map_rows, orbitals, applied_orbitals, t["stick_up"])),
        (pltpu.VMEM((GROUP * PARTS, 128), F32), pltpu.HBM(orbitals.shape, F32)),
        [ANY] * 5,
        (VMEM, ANY),
        [
            pltpu.SMEM(ritz_values.shape, F32),
            pltpu.VMEM(map_rows.shape, jnp.int32),
            pltpu.VMEM(orbitals.shape, F32),
            pltpu.VMEM(orbitals.shape, F32),
            pltpu.VMEM(t["stick_up"].shape, BF16),
            pltpu.VMEM(orbitals.shape, F32),
            pltpu.SemaphoreType.DMA((6,)),
        ],
    )
    received = exchange(sent)
    local, bits, block, place, kept, passed = prepare(ritz_rotation.T, map_rows, orbitals, correction, potential, t)
    came = lax.ppermute(passed, "bg", [(i, i ^ 1) for i in range(4)])
    product, came = lax.optimization_barrier((middle(place, received, local, bits, block, t), came))
    returned = exchange(product)
    last = lax.ppermute(kept[1] + came[1], "bg", [(i, 3 - i) for i in range(4)])
    mine = kept[0] + came[0]
    applied_correction, next_orbitals = call(
        after_kernel,
        "after",
        2,
        tuple(in_vmem(x) for x in (map_rows, correction, returned, t["stick_down"], mine, last)),
        (shape(*orbitals.shape), shape(*orbitals.shape)),
        [VMEM] * 6,
        (VMEM, VMEM),
    )
    return (next_orbitals, applied_correction)


def solution(mesh):
    return jax.shard_map(
        on_device,
        mesh=mesh,
        in_specs=(P("bg", "pw", None), P("bg", "pw", None), P("pw", None, None), P(), P("bg"), P()),
        out_specs=(P("bg", "pw", None), P("bg", "pw", None)),
        check_vma=False,
    )
```

```python
import functools
import math

import jax
import jax.numpy as jnp
import ml_dtypes
import numpy as np
from jax import lax
from jax.experimental import pallas as pl
from jax.experimental.pallas import tpu as pltpu
from jax.sharding import PartitionSpec as P

F32 = jnp.float32
BF16 = jnp.bfloat16
VMEM = pl.BlockSpec(memory_space=pltpu.VMEM)
SMEM = pl.BlockSpec(memory_space=pltpu.SMEM)
ANY = pl.BlockSpec(memory_space=pl.ANY)
PARAMS = pltpu.CompilerParams(vmem_limit_bytes=32 * 1024 * 1024)

LENGTH = 320
WIDTH = 128
FINE = 2 * WIDTH
GROUP = 64
PLANES = LENGTH // GROUP
PARTS = 2 * PLANES
STICKS = GROUP * 64
BANDS = 2


def split_host(table):
    high = table.astype(ml_dtypes.bfloat16)
    low = (table - high.astype(np.float64)).astype(ml_dtypes.bfloat16)
    return high, low


HALF = WIDTH // 2


def frequency_slots():
    return np.concatenate([np.arange(HALF), [-HALF], -np.arange(1, HALF)])


def point_slots():
    return np.concatenate([np.arange(WIDTH), [WIDTH], -np.arange(1, WIDTH)])


def complex_table(frequencies, points, length):
    angles = 2.0 * math.pi * (np.outer(frequencies, points) % length) / length
    cosine, sine = np.cos(angles) / math.sqrt(length), np.sin(angles) / math.sqrt(length)
    return np.concatenate(
        [np.concatenate([cosine, sine], 1), np.concatenate([-sine, cosine], 1)], 0
    )


def wave(function, frequencies, points):
    angles = 2.0 * math.pi * (np.outer(frequencies, points) % FINE) / FINE
    return function(angles) / math.sqrt(FINE)


def folded_tables():
    zeros = np.zeros
    pairs, near = np.arange(HALF), np.arange(WIDTH)
    three = np.concatenate

    def joined(main, single):
        high, low = split_host(main)
        return three([high, high, low, single.astype(ml_dtypes.bfloat16)], 1)

    points = point_slots()
    sines = -wave(np.sin, pairs, points)
    sines[0] = wave(np.sin, [HALF], points)
    single = zeros((FINE, WIDTH))
    single[:, 0] = single[:, HALF] = wave(np.cos, [HALF], points)[0]
    row_up = joined(three([wave(np.cos, pairs, points), sines], 0).T, single).T
    single = zeros((WIDTH + 16, 16))
    single[: WIDTH + 1, 0] = single[: WIDTH + 1, 8] = wave(np.cos, [HALF], np.arange(WIDTH + 1))[0]
    even = zeros((WIDTH + 16, HALF))
    even[: WIDTH + 1] = wave(np.cos, pairs, np.arange(WIDTH + 1)).T
    even_up = joined(even, single)
    single = zeros((WIDTH, 16))
    single[:, 0] = single[:, 8] = -wave(np.sin, [HALF], near)[0]
    odd_up = joined(wave(np.sin, pairs, near).T, single)
    single = zeros((HALF + 16, 16))
    single[: HALF + 1, 0] = single[: HALF + 1, 8] = wave(np.cos, np.arange(HALF + 1), [WIDTH])[:, 0]
    even = zeros((HALF + 16, WIDTH))
    even[: HALF + 1] = wave(np.cos, np.arange(HALF + 1), near)
    even_down = joined(even, single)
    odd_high, odd_low = split_host(wave(np.sin, [HALF, *range(1, HALF)], near))
    odd_down = three([odd_high, odd_high, odd_low], 1)
    return dict(row_up=row_up, even_up=even_up, odd_up=odd_up, even_down=even_down, odd_down=odd_down)


def resampling_table():
    places = point_slots()[:, None] * LENGTH - np.arange(LENGTH)[None, :] * FINE
    total = np.zeros((FINE, LENGTH))
    for d in range(-(WIDTH - 1), WIDTH):
        total += np.cos(2.0 * math.pi * ((places * d) % (FINE * LENGTH)) / (FINE * LENGTH))
    return total / LENGTH


def spreading_table():
    table = np.zeros((2, 2, 8, 16, 8, 4, 2, 16))
    for b in range(2):
        for k in range(8):
            for part in range(16):
                table[b, :, k, part, k, :, b, part] = 1.0
    return table.reshape(512, 1024).astype(ml_dtypes.bfloat16)


def tables():
    high, low = split_host(complex_table(frequency_slots(), point_slots(), FINE))
    stick = complex_table(np.arange(WIDTH) - HALF, np.arange(LENGTH), LENGTH).reshape(2 * WIDTH, 2, GROUP, PLANES)
    stick = stick.transpose(0, 2, 1, 3).reshape(2 * WIDTH, GROUP * PARTS)
    s_high, s_low = split_host(stick)
    r_high, r_low = split_host(resampling_table())
    three = np.concatenate
    return dict(
        **folded_tables(),
        row_down=three([high.T, high.T, low.T], 0),
        stick_up=three([s_high.T, s_low.T], 1),
        stick_down=three([s_high, s_low, s_high], 1),
        fine_cols=three([r_high, r_low, r_high, np.zeros((FINE, 64), r_high.dtype)], 1),
        spread=spreading_table(),
        same=np.tile(np.eye(128), (1, 2)).astype(ml_dtypes.bfloat16),
        fine_rows=three(
            [
                *(r.T[:FINE] for r in (r_high, r_high, r_low)),
                *(r.T[FINE:] for r in (r_high, r_high, r_low)),
                np.zeros((64, FINE), r_high.dtype),
            ],
            0,
        ),
    )


def halves(x):
    high = x.astype(BF16)
    low = (x - high.astype(F32)).astype(BF16)
    return high, low


def data_rows(x, axis):
    high, low = halves(x)
    return jnp.concatenate([high, high, low] if axis == 0 else [high, low, high], axis)


def dot(a, b):
    return jnp.dot(a, b, preferred_element_type=F32)


def slot_of(index):
    return jnp.where(index >= HALF, index - HALF, HALF + ((HALF - index) & (HALF - 1)))


def bare_first(x):
    first = lax.broadcasted_iota(jnp.int32, (8, 1), 0) == 0
    return jnp.concatenate([jnp.where(first, 0.0, x[:8]), x[8:]], 0)


def other_first(x, other):
    first = lax.broadcasted_iota(jnp.int32, (8, 1), 0) == 0
    return jnp.concatenate([jnp.where(first, other[:8], x[:8]), x[8:]], 0)


def folded_data(x, single=None):
    high, low = halves(x)
    parts = [high, low, high]
    if single is not None:
        top = single[:8]
        top_high = top.astype(BF16).astype(F32)
        parts.append(jnp.concatenate([top_high, top - top_high], 0).astype(BF16))
    return jnp.concatenate(parts, 0)


def planar_of(map_ref, sticks):
    me = lax.axis_index("pw")
    per_row = 128 // sticks
    row = map_ref[pl.ds(me // per_row, 1), :]
    fx = (row >> 7) - WIDTH // 2
    fy = (row & (WIDTH - 1)) - WIDTH // 2
    planar = (fx * fx + fy * fy).astype(F32)
    turned = jnp.broadcast_to(planar, (128, 128)).T
    upper = lax.rem(me, per_row) == 1
    return jnp.where(upper, turned[sticks:], turned[:sticks])


def kinetic_of(map_ref, sticks):
    planar = planar_of(map_ref, sticks)
    fz = lax.broadcasted_iota(jnp.int32, (1, WIDTH), 1) - WIDTH // 2
    return (planar + (fz * fz).astype(F32)) * (1.0 / (WIDTH // 2) ** 2)


def before_kernel(
    values_hbm, map_hbm, orb_hbm, app_hbm, up_hbm, send_ref, corr_hbm,
    values_ref, map_ref, orb_ref, app_ref, up_ref, corr_ref, sems,
):
    pairs = (
        (values_hbm, values_ref),
        (map_hbm, map_ref),
        (orb_hbm, orb_ref),
        (app_hbm, app_ref),
        (up_hbm, up_ref),
        (corr_ref, corr_hbm),
    )
    copies = [pltpu.make_async_copy(source, target, sems.at[i]) for i, (source, target) in enumerate(pairs)]
    for copy in copies[:5]:
        copy.start()
    for copy in copies[:4]:
        copy.wait()
    sticks = orb_ref.shape[1]
    kinetic = kinetic_of(map_ref, sticks)
    scale = 1.0 + jnp.concatenate([kinetic, kinetic], 1)
    corr = []
    for b in range(BANDS):
        c = (app_ref[b] - values_ref[b] * orb_ref[b]) / scale
        corr_ref[b] = c
        corr.append(c)
    copies[5].start()
    rows = jnp.concatenate(corr, 0)
    turned = jnp.concatenate([rows[:, :128].T, rows[:, 128:].T], 0)
    high, low = halves(turned)
    copies[4].wait()
    both = jnp.concatenate([high, high], 0)
    for at in range(0, GROUP * PARTS, 160):
        send_ref[at : at + 160, :] = dot(up_ref[at : at + 160, :], both) + dot(up_ref[at : at + 160, : 2 * WIDTH], low)
    copies[5].wait()


def prepare_kernel(
    rotation_hbm, map_hbm, orb_hbm, corr_hbm, pot_hbm, rows_hbm, cols_hbm, out_ref, bits_ref, block_ref, place_ref, keep_ref, pass_ref,
    rotation_ref, map_ref, orb_ref, corr_ref, pot_ref, rows_ref, cols_ref, work_ref, sems,
):
    pairs = [
        (rotation_hbm, rotation_ref),
        (map_hbm, map_ref),
        (orb_hbm, orb_ref),
        (corr_hbm, corr_ref),
        (rows_hbm, rows_ref),
        *((pot_hbm.at[p], pot_ref.at[p]) for p in range(PLANES)),
        (cols_hbm, cols_ref),
    ]
    copies = [pltpu.make_async_copy(source, target, sems.at[i]) for i, (source, target) in enumerate(pairs)]
    for copy in copies:
        copy.start()
    for p in range(PLANES):
        work_ref[p, 3 * LENGTH :] = jnp.zeros((64, FINE), BF16)
    for copy in copies[:4]:
        copy.wait()
    me = lax.axis_index("bg")
    all_bands = rotation_ref.shape[0]
    for target, group in ((keep_ref, me), (pass_ref, me ^ 1)):
        for k, owner in enumerate((group, 3 - group)):
            for i in range(BANDS):
                j = owner * BANDS + i
                total = None
                for b in range(BANDS):
                    term = rotation_ref[j, me * BANDS + b] * orb_ref[b]
                    term = term + rotation_ref[j, all_bands + me * BANDS + b] * corr_ref[b]
                    total = term if total is None else total + term
                target[k, i] = total
    columns = slot_of(map_ref[...] >> 7)
    place_ref[...] = ((columns >> 2) << 7) | slot_of(map_ref[...] & 127)
    columns = columns & 3
    block_ref[...] = columns
    row_block = lax.broadcasted_iota(jnp.int32, (128, 128), 0) >> 5
    stick = lax.broadcasted_iota(jnp.int32, (16, 128), 1)
    eight = lax.broadcasted_iota(jnp.int32, (16, 128), 0)
    weights = jnp.where((stick >> 3) == eight, (1 << (stick & 7)).astype(F32), 0.0).astype(BF16)
    marked = 0
    copies[4].wait()
    for p in range(PLANES):
        copies[5 + p].wait()
        for at in range(0, LENGTH, LENGTH // 2):
            end = at + LENGTH // 2
            high, low = halves(pot_ref[p, at:end, :FINE])
            rest = pot_ref[p, at:end, FINE:]
            rest_high = rest.astype(BF16).astype(F32)
            rest = jnp.concatenate([rest_high, rest - rest_high, rest_high, jnp.zeros_like(rest)], 1)
            part = dot(jnp.concatenate([high, low, high, rest.astype(BF16)], 1), rows_ref[...])
            high, low = halves(part)
            for k, values in enumerate((high, high, low)):
                work_ref[p, k * LENGTH + at : k * LENGTH + end] = values
            for _ in range(4):
                if marked < STICKS // 128:
                    match = jnp.where(columns[marked : marked + 1, :] == row_block, 1.0, 0.0).astype(BF16)
                    bits = lax.dot_general(weights, match, (((1,), (1,)), ((), ())), preferred_element_type=F32)
                    bits_ref[marked * 16 : marked * 16 + 16, :] = bits.astype(jnp.int32)
                    marked += 1
        if p == 0:
            copies[5 + PLANES].wait()
        out_ref[p] = dot(cols_ref[...], work_ref[p])


def across(same, x):
    both = jnp.concatenate(halves(x), 1)
    return lax.dot_general(same[...], both, (((1,), (1,)), ((), ())), preferred_element_type=F32)


def middle_kernel(
    place_hbm, recv_ref, pot_ref, bits_ref, block_hbm, spread_hbm, row_up_hbm, even_up_hbm, odd_up_hbm, even_down_hbm,
    odd_down_hbm, row_down_hbm, same_hbm,
    send_hbm,
    send_ref, place_ref, block_ref, sticks_ref, square_ref, turned_ref, rows_ref, half_ref, back_ref,
    spread, row_up, even_up, odd_up, even_down, odd_down, row_down, same, sems,
):
    copies = [
        pltpu.make_async_copy(source, target, sems.at[i])
        for i, (source, target) in enumerate(
            (
                (spread_hbm, spread),
                (place_hbm, place_ref),
                (row_up_hbm, row_up),
                (even_up_hbm, even_up),
                (odd_up_hbm, odd_up),
                (even_down_hbm, even_down),
                (odd_down_hbm, odd_down),
                (row_down_hbm, row_down),
                (same_hbm, same),
                (block_hbm, block_ref),
            )
        )
    ]
    for copy in copies:
        copy.start()
    square_ref[...] = jnp.zeros_like(square_ref)
    lane = lax.broadcasted_iota(jnp.int32, (1, 128), 1)

    for g in range(GROUP // 8):
        parts = []
        for d in range(8 * g, 8 * g + 8):
            parts += [recv_ref[d * PARTS : d * PARTS + 8, :], recv_ref[d * PARTS + 2 : d * PARTS + 10, :]]
        turned = jnp.concatenate(parts, 0).T
        first, second = halves(turned[:64]), halves(turned[64:])
        rows_ref[g * 64 : g * 64 + 64, :512] = jnp.concatenate([*first, *second], 1)
    copies[0].wait()
    for g in range(0, GROUP // 8, 4):
        found = dot(rows_ref[g * 64 : g * 64 + 256, :512], spread[...])
        for h in range(4):
            for k in range(8):
                at = (8 * (g + h) + k) * 64
                sticks_ref[at : at + 64, :] = found[h * 64 : h * 64 + 64, k * 128 : k * 128 + 128]
    copies[1].wait()

    def scatter(i, _):
        first = pl.multiple_of(i * 128, 128)
        for j in range(128):
            pltpu.store(
                square_ref.at[pl.ds(place_ref[i, j], 1), :],
                sticks_ref[pl.ds(first + j, 1), :],
                mask=(bits_ref[pl.ds(i * 16 + j // 8, 1), :] & (1 << (j % 8))) != 0,
            )
        return 0

    lax.fori_loop(0, STICKS // 128, scatter, 0)

    for at in range(0, STICKS, 128):
        turned_ref[at : at + 128, :] = square_ref[at : at + 128, :].T
    pairs = [(b, p) for b in range(BANDS) for p in range(PLANES)]
    copies[2].wait()
    left = lane < HALF
    alone = (lane & (HALF - 1)) == 0
    for k, (b, p) in enumerate(pairs):
        sums = []
        ends = []
        for at in (b * 16 + p, b * 16 + 8 + 3 + p):
            x = turned_ref[pl.ds(at, 128, stride=32), :]
            mirror = pltpu.roll(x, HALF, 1)
            sums.append(jnp.where(alone, x, jnp.where(left, x, -x) + mirror))
            end = jnp.where(left, mirror, x)
            end_high = end.astype(BF16).astype(F32)
            ends.append(jnp.where(left, end - end_high, end_high).astype(BF16))
        real, imag = sums
        for i, x in enumerate((jnp.where(left, real, imag), jnp.where(left, imag, -real))):
            high, low = halves(x)
            rows_ref[k * 128 : k * 128 + 128, i * 512 : i * 512 + 512] = jnp.concatenate([high, low, high, ends[i]], 1)
        if k % 2 == 1:
            at = (k - 1) * 128
            for i in range(2):
                half_ref[at : at + 256, i * FINE : i * FINE + FINE] = dot(
                    rows_ref[at : at + 256, i * 512 : i * 512 + 512], row_up[...]
                )
    for copy in copies[3:]:
        copy.wait()
    for k, (b, p) in enumerate(pairs):
        upper = half_ref[k * 128 : k * 128 + HALF, :]
        lower = half_ref[k * 128 + HALF : k * 128 + 128, :]
        even = dot(even_up[...], folded_data(upper + bare_first(lower), lower))
        odd = dot(odd_up[...], folded_data(upper - lower, lower))
        odd_real, odd_imag = odd[:, :FINE], odd[:, FINE:]
        local = pot_ref[p]
        last = even[WIDTH : WIDTH + 8]
        even = even[:WIDTH]
        ahead = jnp.concatenate([even[:, :FINE] - odd_imag, even[:, FINE:] + odd_real], 1)
        behind = jnp.concatenate([even[:, :FINE] + odd_imag, even[:, FINE:] - odd_real], 1)
        behind = other_first(behind, last)
        ahead = ahead * jnp.concatenate([local[:WIDTH], local[:WIDTH]], 1)
        behind = behind * jnp.concatenate([local[WIDTH:], local[WIDTH:]], 1)
        even = dot(even_down[...], folded_data(ahead + bare_first(behind), behind))
        odd = dot(odd_down[...], folded_data(ahead - behind))
        odd_plus = bare_first(odd)
        last = even[HALF : HALF + 8]
        even = even[:HALF]
        even_minus = other_first(even, last)
        real = jnp.concatenate(
            [even[:, :FINE] + odd_plus[:, FINE:], even_minus[:, :FINE] - odd[:, FINE:]], 0
        )
        imag = jnp.concatenate(
            [even[:, FINE:] - odd_plus[:, :FINE], even_minus[:, FINE:] + odd[:, :FINE]], 0
        )
        rows_ref[k * 128 : k * 128 + 128, :] = data_rows(jnp.concatenate([real, imag], 1), 1)
        if k % 2 == 1:
            at = (k - 1) * 128
            back_ref[at : at + 256, :] = dot(rows_ref[at : at + 256, :], row_down[...])
    for k, (b, p) in enumerate(pairs):
        for c in range(2):
            turned_ref[pl.ds(b * 16 + c * 8 + p, 128, stride=32), :] = back_ref[
                k * 128 : k * 128 + 128, c * 128 : c * 128 + 128
            ]

    for at in range(0, STICKS, 128):
        square_ref[at : at + 128, :] = turned_ref[at : at + 128, :].T

    def gather(i, _):
        first = pl.multiple_of(i * 128, 128)
        for j in range(128):
            sticks_ref[pl.ds(first + j, 1), :] = square_ref[pl.ds(place_ref[i, j], 1), :]
        return 0

    lax.fori_loop(0, STICKS // 128, gather, 0)
    sent = []
    left = lane < 64
    for at in range(0, STICKS, 256):
        every = across(same, sticks_ref[at : at + 256, :])
        own = jnp.concatenate([block_ref[at // 128 + i : at // 128 + i + 1, :] for i in range(2)], 1)
        found = every[:32]
        for h in range(1, 4):
            found = jnp.where(own == h, every[32 * h : 32 * h + 32], found)
        for h in range(2):
            here = found[:, h * 128 : h * 128 + 128]
            swapped = pltpu.roll(here, 64, 1)
            for i, part in enumerate(
                (jnp.where(left, here[:16], swapped[16:]), jnp.where(left, swapped[:16], here[16:]))
            ):
                to = (at // 64 + 2 * h + i) * PARTS
                send_ref[to : to + PLANES, :] = part[:PLANES]
                send_ref[to + PLANES : to + PARTS, :] = part[8 : 8 + PLANES]
        if at % 1024 == 768:
            part = pl.ds((at - 768) // 64 * PARTS, 16 * PARTS)
            sent.append(pltpu.make_async_copy(send_ref.at[part, :], send_hbm.at[part, :], sems.at[10 + len(sent)]))
            sent[-1].start()
    for copy in sent:
        copy.wait()


def after_kernel(map_ref, corr_ref, recv_ref, down_ref, mine_ref, last_ref, out_ref, next_ref):
    sticks = corr_ref.shape[1]
    kinetic = kinetic_of(map_ref, sticks)
    local = dot(down_ref[...], data_rows(recv_ref[...], 0))
    local = jnp.concatenate([local[:128].T, local[128:].T], 1)
    both = jnp.concatenate([kinetic, kinetic], 1)
    for b in range(BANDS):
        out_ref[b] = both * corr_ref[b] + local[b * sticks : (b + 1) * sticks]
        next_ref[b] = mine_ref[b] + last_ref[b]


def shape(*dims):
    return jax.ShapeDtypeStruct(dims, F32)


def exchange(values):
    values = values.reshape(GROUP, 1, PARTS * 128)
    return lax.all_to_all(values, "pw", 0, 0, tiled=True).reshape(GROUP * PARTS, 128)


def in_vmem(x):
    return pltpu.with_memory_space_constraint(x, pltpu.VMEM)


def in_hbm(x):
    return pltpu.with_memory_space_constraint(x, pltpu.HBM)


def cost(us):
    return pl.CostEstimate(flops=int(us * 1e9), bytes_accessed=int(us * 3e6), transcendentals=0)


def call(kernel, name, us, inputs, out_shape, in_specs, out_specs, scratch=()):
    return pl.pallas_call(
        kernel,
        out_shape=out_shape,
        in_specs=in_specs,
        out_specs=out_specs,
        scratch_shapes=list(scratch),
        compiler_params=PARAMS,
        cost_estimate=cost(us),
        name=name,
    )(*inputs)


def middle(place, received, local, bits, block, t):
    grid = BANDS * PLANES * 128
    names = ("spread", "row_up", "even_up", "odd_up", "even_down", "odd_down", "row_down", "same")
    return call(
        middle_kernel,
        "middle",
        20,
        (in_hbm(place), in_vmem(received), in_vmem(local), in_vmem(bits), in_hbm(block), *(in_hbm(t[n]) for n in names)),
        pltpu.HBM((GROUP * PARTS, 128), F32),
        [ANY] + [VMEM] * 3 + [ANY] * 9,
        ANY,
        [
            pltpu.VMEM((GROUP * PARTS, 128), F32),
            pltpu.SMEM((STICKS // 128, 128), jnp.int32),
            pltpu.VMEM((STICKS // 128, 128), jnp.int32),
            pltpu.VMEM((STICKS, 128), F32),
            pltpu.VMEM((STICKS, 128), F32),
            pltpu.VMEM((STICKS, 128), F32),
            pltpu.VMEM((grid, 6 * FINE), BF16),
            pltpu.VMEM((grid, 2 * FINE), F32),
            pltpu.VMEM((grid, FINE), F32),
            *(pltpu.VMEM(t[n].shape, BF16) for n in names),
            pltpu.SemaphoreType.DMA((14,)),
        ],
    )


def prepare(rotation, map_rows, orbitals, correction, potential, t):
    bands, sticks, doubled = orbitals.shape
    return call(
        prepare_kernel,
        "prepare",
        7,
        tuple(
            in_hbm(x)
            for x in (rotation, map_rows, orbitals, correction, potential, t["fine_rows"], t["fine_cols"])
        ),
        (
            pltpu.VMEM((PLANES, FINE, FINE), F32),
            pltpu.VMEM((STICKS // 8, 128), jnp.int32),
            pltpu.HBM(map_rows.shape, jnp.int32),
            pltpu.HBM(map_rows.shape, jnp.int32),
            pltpu.VMEM((2, BANDS, sticks, doubled), F32),
            pltpu.HBM((2, BANDS, sticks, doubled), F32),
        ),
        [ANY] * 7,
        (VMEM,) * 6,
        [
            pltpu.SMEM(rotation.shape, F32),
            pltpu.VMEM(map_rows.shape, jnp.int32),
            pltpu.VMEM(orbitals.shape, F32),
            pltpu.VMEM(orbitals.shape, F32),
            pltpu.VMEM((PLANES, LENGTH, LENGTH), F32),
            pltpu.VMEM(t["fine_rows"].shape, BF16),
            pltpu.VMEM(t["fine_cols"].shape, BF16),
            pltpu.VMEM((PLANES, 3 * LENGTH + 64, FINE), BF16),
            pltpu.SemaphoreType.DMA((PLANES + 6,)),
        ],
    )


def on_device(orbitals, applied_orbitals, potential, stick_map, ritz_values, ritz_rotation):
    t = {name: jnp.asarray(value) for name, value in tables().items()}
    map_rows = stick_map.reshape(-1, 128)
    sent, correction = call(
        before_kernel,
        "before",
        2,
        tuple(in_hbm(x) for x in (ritz_values, map_rows, orbitals, applied_orbitals, t["stick_up"])),
        (pltpu.VMEM((GROUP * PARTS, 128), F32), pltpu.HBM(orbitals.shape, F32)),
        [ANY] * 5,
        (VMEM, ANY),
        [
            pltpu.SMEM(ritz_values.shape, F32),
            pltpu.VMEM(map_rows.shape, jnp.int32),
            pltpu.VMEM(orbitals.shape, F32),
            pltpu.VMEM(orbitals.shape, F32),
            pltpu.VMEM(t["stick_up"].shape, BF16),
            pltpu.VMEM(orbitals.shape, F32),
            pltpu.SemaphoreType.DMA((6,)),
        ],
    )
    received = exchange(sent)
    local, bits, block, place, kept, passed = prepare(ritz_rotation.T, map_rows, orbitals, correction, potential, t)
    came = lax.ppermute(passed, "bg", [(i, i ^ 1) for i in range(4)])
    product, came = lax.optimization_barrier((middle(place, received, local, bits, block, t), came))
    returned = exchange(product)
    last = lax.ppermute(kept[1] + came[1], "bg", [(i, 3 - i) for i in range(4)])
    mine = kept[0] + came[0]
    applied_correction, next_orbitals = call(
        after_kernel,
        "after",
        2,
        tuple(in_vmem(x) for x in (map_rows, correction, returned, t["stick_down"], mine, last)),
        (shape(*orbitals.shape), shape(*orbitals.shape)),
        [VMEM] * 6,
        (VMEM, VMEM),
    )
    return (next_orbitals, applied_correction)


def solution(mesh):
    return jax.shard_map(
        on_device,
        mesh=mesh,
        in_specs=(P("bg", "pw", None), P("bg", "pw", None), P("pw", None, None), P(), P("bg"), P()),
        out_specs=(P("bg", "pw", None), P("bg", "pw", None)),
        check_vma=False,
    )
```
